512 devices in a mesh: space: 64 (over x, z, y_lo), rep: 8 (over y_hi, core).
Axes of the slice: x: 4, y: 8 (y_hi: 4, y_lo: 2; y = y_hi * 2 + y_lo), z: 8, core: 2. Of those that a mesh axis runs over, the one named last changes fastest.
Arguments:
- voxels: bfloat16 [8, 128, 8, 8, 8, 96], P('rep', 'space'), may hold values from -6 to 6
- cotangent: bfloat16 [8, 128, 8, 8, 8, 96], P('rep', 'space'), may hold values from -6 to 6
- weight_first: bfloat16 [27, 96, 96], replicated, may hold values from -0.125 to 0.125
- weight_second: bfloat16 [27, 96, 96], replicated, may hold values from -0.125 to 0.125
- act_count: int32 [8, 64], P('rep', 'space'), may hold values from 1 to 2, as said below
- up_list: int32 [8, 64], P('rep', 'space'), may hold values from 0 to 2, as said below
- down_list: int32 [8, 64], P('rep', 'space'), may hold values from 0 to 2, as said below
- table: int32 [8, 128, 9], P('rep', 'space'), may hold values from 0 to 3, as said below
Outputs:
- out_field: bfloat16 [8, 128, 8, 8, 8, 96], P('rep', 'space')
- grad_first: float32 [27, 96, 96], replicated
- grad_second: float32 [27, 96, 96], replicated
The draws below stay inside these ranges and needn't reach their ends.
Inputs may be any that keep to these rules, and one draw needn't show every extreme that they name: Slots 0 to act_count - 1 of an owner hold its active bricks. In every tile one owner holds 2 active bricks and every other owner at most 1. `up_list`: entry r is the slot of the owner's r-th active brick at local brick x = 1, in increasing y; 2 after the last one. `down_list`: entry r is the slot of the owner's r-th active brick at local brick x = 0, in increasing y; 2 after the last one. `table`: slot p of an owner at local brick position (x, y), x in 0..1, y in 0..0, and direction (dx, dy): the neighbouring position's active brick within the owner (its slot), or in owner o-1 (dx = -1) or o+1 (dx = +1) as 2 + its rank in that owner's up_list or down_list; 3 where no active brick is there, outside the tile, or beyond the first and last owner. Each tile is one brick high.
All inputs are finite; a program needn't handle non-finite values.
Results may differ from the reference program's by a relative error of at most 0.0029.
Values may be sent and summed in bfloat16 or wider, within the bound.
A program may use at most 128 MiB of HBM per device.

```python
import math
import jax
import jax.numpy as jnp
from jax import lax

CHANNELS = 96
BRICK = 8
ROWS_Y = 1
SLOTS = 2
FACE_CAP = 1
OWNERS = 64
TILES = 8


def brick_layout(key):
    key_count, key_full, key_order = jax.random.split(key, 3)
    counts = jax.random.randint(key_count, (TILES, OWNERS), 1, ROWS_Y + 1)
    full_owner = jax.random.randint(key_full, (TILES, 1), 0, OWNERS)
    counts = jnp.where(jnp.arange(OWNERS)[None, :] == full_owner, SLOTS, counts).astype(jnp.int32)
    scores = jax.random.randint(key_order, (TILES, OWNERS, SLOTS), 0, 1 << 20) * SLOTS + jnp.arange(SLOTS)[None, None, :]
    placed = jnp.argsort(scores, axis=-1).astype(jnp.int32)
    live = jnp.arange(SLOTS)[None, None, :] < counts[:, :, None]
    pairing = (placed[:, :, :, None] == jnp.arange(SLOTS)[None, None, None, :]) & live[:, :, :, None]
    filled = jnp.any(pairing, axis=2)
    holder = jnp.sum(pairing.astype(jnp.int32) * jnp.arange(SLOTS)[:, None], axis=2).astype(jnp.int32)
    return (counts, placed, filled, holder)


def face_list(filled_row, holder_row):
    flags = filled_row.astype(jnp.int32)
    face_rank = jnp.cumsum(flags, axis=-1) - flags
    chosen = filled_row[:, :, None, :] & (face_rank[:, :, None, :] == jnp.arange(FACE_CAP)[:, None])
    listing = jnp.where(jnp.any(chosen, axis=-1), jnp.sum(chosen.astype(jnp.int32) * holder_row[:, :, None, :], axis=-1), SLOTS)
    return (listing.astype(jnp.int32), face_rank.astype(jnp.int32))


def draw_act_count(key, part):
    counts, placed, filled, holder = brick_layout(key)
    return counts


def draw_up_list(key, part):
    counts, placed, filled, holder = brick_layout(key)
    filled_grid = filled.reshape(TILES, OWNERS, 2, ROWS_Y)
    holder_grid = holder.reshape(TILES, OWNERS, 2, ROWS_Y)
    listing, face_rank = face_list(filled_grid[:, :, 1], holder_grid[:, :, 1])
    return listing.reshape(TILES, OWNERS * FACE_CAP)


def draw_down_list(key, part):
    counts, placed, filled, holder = brick_layout(key)
    filled_grid = filled.reshape(TILES, OWNERS, 2, ROWS_Y)
    holder_grid = holder.reshape(TILES, OWNERS, 2, ROWS_Y)
    listing, face_rank = face_list(filled_grid[:, :, 0], holder_grid[:, :, 0])
    return listing.reshape(TILES, OWNERS * FACE_CAP)


def draw_table(key, part):
    counts, placed, filled, holder = brick_layout(key)
    filled_grid = filled.reshape(TILES, OWNERS, 2, ROWS_Y)
    holder_grid = holder.reshape(TILES, OWNERS, 2, ROWS_Y)
    up_listing, up_rank = face_list(filled_grid[:, :, 1], holder_grid[:, :, 1])
    down_listing, down_rank = face_list(filled_grid[:, :, 0], holder_grid[:, :, 0])
    absent = SLOTS + FACE_CAP
    no_face = jnp.zeros((TILES, 1, ROWS_Y), bool)
    no_rank = jnp.zeros((TILES, 1, ROWS_Y), jnp.int32)
    lower_filled = jnp.concatenate([no_face, filled_grid[:, :-1, 1]], axis=1)
    lower_rank = jnp.concatenate([no_rank, up_rank[:, :-1]], axis=1)
    upper_filled = jnp.concatenate([filled_grid[:, 1:, 0], no_face], axis=1)
    upper_rank = jnp.concatenate([down_rank[:, 1:], no_rank], axis=1)
    pos_x = placed // ROWS_Y
    pos_y = placed % ROWS_Y
    entries = []
    for step_x in (-1, 0, 1):
        for step_y in (-1, 0, 1):
            near_y = pos_y + step_y
            inside = (near_y >= 0) & (near_y < ROWS_Y)
            clipped = jnp.clip(near_y, 0, ROWS_Y - 1)
            near_x = pos_x + step_x
            spot_index = jnp.clip(near_x, 0, 1) * ROWS_Y + clipped
            local_ok = jnp.take_along_axis(filled, spot_index, axis=-1)
            local_value = jnp.take_along_axis(holder, spot_index, axis=-1)
            lower_ok = jnp.take_along_axis(lower_filled, clipped, axis=-1)
            lower_value = SLOTS + jnp.take_along_axis(lower_rank, clipped, axis=-1)
            upper_ok = jnp.take_along_axis(upper_filled, clipped, axis=-1)
            upper_value = SLOTS + jnp.take_along_axis(upper_rank, clipped, axis=-1)
            entry_value = jnp.where(local_ok, local_value, absent)
            entry_value = jnp.where(near_x < 0, jnp.where(lower_ok, lower_value, absent), entry_value)
            entry_value = jnp.where(near_x > 1, jnp.where(upper_ok, upper_value, absent), entry_value)
            entries.append(jnp.where(inside, entry_value, absent).astype(jnp.int32))
    return jnp.stack(entries, axis=-1).reshape(TILES, OWNERS * SLOTS, 9)


def shard_levels(own_key, extent, cuts, low, largest):
    def one(axis_at, parts):
        steps = jax.random.uniform(jax.random.fold_in(jax.random.fold_in(own_key, 6), axis_at), (parts,), jnp.float32, low / len(cuts), largest / len(cuts))
        return jnp.repeat(jnp.exp(steps), extent[axis_at] // parts).reshape((-1,) + (1,) * (len(extent) - axis_at - 1))

    factor_of = one(*cuts[0])
    for cut in cuts[1:]:
        factor_of = factor_of * one(*cut)
    return factor_of


def noise(key, dims, scale, reach, shards=(), held_as=jnp.bfloat16):
    values = jax.random.normal(key, dims, jnp.float32) * scale
    if len(shards) > 0:
        values = shard_levels(key, dims, shards, -0.22, 0.18) * values
    return jnp.clip(values, min=-reach, max=reach).astype(held_as)


def setup_inputs(seed: int = 0) -> dict:
    seeds = jax.random.split(jax.random.key(seed), 9)
    return {
        "voxels": noise(seeds[0], (TILES, OWNERS * SLOTS, BRICK, BRICK, BRICK, CHANNELS), 1.0, 6.0, ((0, 8), (1, 64))),
        "cotangent": noise(seeds[1], (TILES, OWNERS * SLOTS, BRICK, BRICK, BRICK, CHANNELS), 1.0, 6.0, ((0, 8), (1, 64))),
        "weight_first": noise(seeds[2], (27, CHANNELS, CHANNELS), (27 * CHANNELS) ** -0.5, 0.125),
        "weight_second": noise(seeds[3], (27, CHANNELS, CHANNELS), (27 * CHANNELS) ** -0.5, 0.125),
        "act_count": draw_act_count(jax.random.fold_in(seeds[8], 71), 0),
        "up_list": draw_up_list(jax.random.fold_in(seeds[8], 71), 0),
        "down_list": draw_down_list(jax.random.fold_in(seeds[8], 71), 0),
        "table": draw_table(jax.random.fold_in(seeds[8], 71), 0),
    }


def face_planes(field, plane, listing):
    blank_row = jnp.zeros((1,) + field.shape[2:], field.dtype)
    return jnp.take(jnp.concatenate([field[:, plane], blank_row], axis=0), listing, axis=0)

def assemble(field, from_lower, from_upper, links):
    brick_edge = field.shape[1]
    x_blocks = []
    for step_x in (-1, 0, 1):
        y_blocks = []
        for step_y in (-1, 0, 1):
            y_start, y_stop = ((brick_edge - 1, brick_edge), (0, brick_edge), (0, 1))[step_y + 1]
            if step_x == 0:
                own_piece = field[:, :, y_start:y_stop]
                far_piece = jnp.zeros((from_lower.shape[0],) + own_piece.shape[1:], field.dtype)
            elif step_x < 0:
                own_piece = field[:, brick_edge - 1:brick_edge, y_start:y_stop]
                far_piece = from_lower[:, None, y_start:y_stop]
            else:
                own_piece = field[:, 0:1, y_start:y_stop]
                far_piece = from_upper[:, None, y_start:y_stop]
            blank_row = jnp.zeros((1,) + own_piece.shape[1:], field.dtype)
            sources = jnp.concatenate([own_piece, far_piece, blank_row], axis=0)
            y_blocks.append(jnp.take(sources, links[:, (step_x + 1) * 3 + step_y + 1], axis=0))
        x_blocks.append(jnp.concatenate(y_blocks, axis=2))
    block = jnp.concatenate(x_blocks, axis=1)
    return jnp.pad(block, ((0, 0), (0, 0), (0, 0), (1, 1), (0, 0)))

def convolve(padded, weight):
    brick_count = padded.shape[0]
    brick_edge = padded.shape[1] - 2
    width_in = padded.shape[-1]
    summed = jnp.zeros((brick_count * brick_edge ** 3, weight.shape[-1]), jnp.float32)
    for offset in range(27):
        offset_x, offset_y, offset_z = (offset // 9, offset // 3 % 3, offset % 3)
        windowed = padded[:, offset_x:offset_x + brick_edge, offset_y:offset_y + brick_edge, offset_z:offset_z + brick_edge]
        summed = summed + jnp.dot(windowed.reshape(-1, width_in), weight[offset], preferred_element_type=jnp.float32)
    return summed.reshape(brick_count, brick_edge, brick_edge, brick_edge, -1)

def weight_terms(padded, grads):
    brick_edge = grads.shape[1]
    width_in = padded.shape[-1]
    flat_grads = grads.reshape(-1, grads.shape[-1])
    terms = []
    for offset in range(27):
        offset_x, offset_y, offset_z = (offset // 9, offset // 3 % 3, offset % 3)
        windowed = padded[:, offset_x:offset_x + brick_edge, offset_y:offset_y + brick_edge, offset_z:offset_z + brick_edge]
        terms.append(lax.dot_general(windowed.reshape(-1, width_in), flat_grads, (((0,), (0,)), ((), ())), preferred_element_type=jnp.float32))
    return jnp.stack(terms)

def silu_slope(value):
    sigmoid = jax.nn.sigmoid(value)
    return sigmoid * (1.0 + value * (1.0 - sigmoid))

def reference(voxels, cotangent, weight_first, weight_second, act_count, up_list, down_list, table):

    def upper_faces(field, listing):
        return face_planes(field, BRICK - 1, listing)

    def lower_faces(field, listing):
        return face_planes(field, 0, listing)

    def neighbourhood(field, upward_list, downward_list, links):
        owners = field.reshape((OWNERS, SLOTS) + field.shape[1:])
        upward = jax.vmap(upper_faces)(owners, upward_list)
        downward = jax.vmap(lower_faces)(owners, downward_list)
        zero_face = jnp.zeros_like(upward[:1])
        from_lower = jnp.concatenate([zero_face, upward[:-1]], axis=0)
        from_upper = jnp.concatenate([downward[1:], zero_face], axis=0)
        padded = jax.vmap(assemble)(owners, from_lower, from_upper, links)
        return padded.reshape((-1,) + padded.shape[2:])

    def one_tile(tile_args):
        tile_voxels, tile_cotangent, counts, upward_list, downward_list, links = tile_args
        upward_list = upward_list.reshape(OWNERS, FACE_CAP)
        downward_list = downward_list.reshape(OWNERS, FACE_CAP)
        links = links.reshape(OWNERS, SLOTS, 9)
        live = jnp.arange(SLOTS, dtype=jnp.int32)[None, :] < counts[:, None]
        live_mask = live.astype(jnp.float32).reshape(-1, 1, 1, 1, 1)
        inputs = tile_voxels * live_mask.astype(jnp.bfloat16)
        x_pad = neighbourhood(inputs, upward_list, downward_list, links)
        before = convolve(x_pad, weight_first) * live_mask
        hidden = jax.nn.silu(before).astype(jnp.bfloat16)
        h_pad = neighbourhood(hidden, upward_list, downward_list, links)
        out_tile = ((convolve(h_pad, weight_second) + inputs.astype(jnp.float32)) * live_mask).astype(jnp.bfloat16)
        cotangent_live = tile_cotangent * live_mask.astype(jnp.bfloat16)
        g_pad = neighbourhood(cotangent_live, upward_list, downward_list, links)
        second = weight_terms(h_pad, cotangent_live)
        flipped = jnp.swapaxes(weight_second[::-1], 1, 2)
        through = convolve(g_pad, flipped) * live_mask
        slope = (through * silu_slope(before)).astype(jnp.bfloat16)
        first = weight_terms(x_pad, slope)
        return (out_tile, first, second)
    out_field, firsts, seconds = lax.map(one_tile, (voxels, cotangent, act_count, up_list, down_list, table))
    scale = 1.0 / math.sqrt(TILES * OWNERS * SLOTS * BRICK ** 3)
    return (out_field, lax.optimization_barrier(jnp.sum(firsts, axis=0)) * scale, lax.optimization_barrier(jnp.sum(seconds, axis=0)) * scale)
```

```python
import functools
import math

import jax
import jax.numpy as jnp
from jax import lax
from jax.experimental import pallas as pl
from jax.experimental.pallas import tpu as pltpu
from jax.sharding import PartitionSpec as P

F32 = jnp.float32
BF16 = jnp.bfloat16
MESH = pl.DeviceIdType.MESH

SIZE_X, SIZE_Y, SIZE_Z = 4, 8, 8
EDGE = 8
CH = 96
LANES = 128
FACE = EDGE * EDGE
PLANES = 2 * EDGE
ROWS = PLANES * FACE
WIDE = 9 * CH
TILES_WIDE = 7
HALF = 1024
PART = 128
SHARD = 16
CHUNK = 4
STEP = CHUNK * FACE


def widen(value):
    value = value.astype(F32)
    blank = jnp.zeros(value.shape[:-1] + (LANES - CH,), F32)
    return jnp.concatenate([value, blank], axis=-1)


def spread(value, out, row):
    planes = value.shape[0]
    flat = value.reshape(planes * EDGE, EDGE, LANES)
    depth = lax.broadcasted_iota(jnp.int32, flat.shape, 1)
    by_depth = [
        jnp.where(depth == 0, 0.0, pltpu.roll(flat, 1, 1)),
        flat,
        jnp.where(depth == EDGE - 1, 0.0, pltpu.roll(flat, EDGE - 1, 1)),
    ]

    def piece(index):
        shift_y, shift_z = index // 3, index % 3
        turned = by_depth[shift_z]
        turn = CH * index % LANES
        if turn:
            turned = pltpu.roll(turned, turn, 2)
        turned = turned.reshape(planes, EDGE, EDGE, LANES)
        blank = jnp.zeros((planes, 1, EDGE, LANES), F32)
        if shift_y == 0:
            turned = jnp.concatenate([blank, turned[:, : EDGE - 1]], axis=1)
        elif shift_y == 2:
            turned = jnp.concatenate([turned[:, 1:], blank], axis=1)
        return turned.reshape(planes * FACE, LANES)

    lane = lax.broadcasted_iota(jnp.int32, (planes * FACE, LANES), 1)
    pieces = [piece(index) for index in range(9)]
    for tile in range(TILES_WIDE):
        first = LANES * tile // CH
        border = CH * (first + 1) - LANES * tile
        block = pieces[first]
        if border < LANES and first + 1 < 9:
            block = jnp.where(lane < border, block, pieces[first + 1])
        out[pl.ds(row, planes * FACE), LANES * tile : LANES * (tile + 1)] = block.astype(BF16)


def section(
    scale,
    down_ref, up_ref, vox, cot, w1, w2,
    out, packed,
    ax, ah, ag, wa, wb, wt, dslope, sums, st, ct,
    up_send, down_send, from_lo, from_hi, hup_send, hdown_send, hfrom_lo, hfrom_hi,
    part_sum, core_in, ring_out, ring_in, mid, mid_in, cross,
    halo_s, halo_r, s0, r0, s1, r1, s2, r2, s3, r3, s4, r4, s5, r5, s6, r6,
):
    space = lax.axis_index("space")
    rep = lax.axis_index("rep")
    owners = SIZE_X * SIZE_Z * 2
    y_lo = lax.rem(space, 2)
    my_z = lax.rem(lax.div(space, 2), SIZE_Z)
    my_x = lax.div(space, 2 * SIZE_Z)
    core = lax.rem(rep, 2)
    my_y = lax.div(rep, 2) * 2 + y_lo

    def device(x, y, z, c):
        return ((x * SIZE_Z + z) * 2 + lax.rem(y, 2), lax.div(y, 2) * 2 + c)

    pos1 = my_y * (1 - core) + my_z * core
    pos2 = my_z * (1 - core) + my_y * core

    def ring1(t):
        return device(my_x, t * (1 - core) + my_y * core, my_z * (1 - core) + t * core, core)

    def ring2(t):
        return device(my_x, my_y * (1 - core) + t * core, t * (1 - core) + my_z * core, core)

    def across(t):
        return device(t, my_y, my_z, core)

    twin = device(my_x, my_y, my_z, 1 - core)
    above = (lax.rem(space + 1, owners), rep)
    below = (lax.rem(space + owners - 1, owners), rep)

    def send(src, dst, send_sem, recv_sem, target):
        copy = pltpu.make_async_remote_copy(
            src_ref=src, dst_ref=dst, send_sem=send_sem, recv_sem=recv_sem,
            device_id=target, device_id_type=MESH,
        )
        copy.start()
        return copy

    def arrived(dst, send_sem, recv_sem, target):
        pltpu.make_async_remote_copy(
            src_ref=dst, dst_ref=dst, send_sem=send_sem, recv_sem=recv_sem,
            device_id=target, device_id_type=MESH,
        ).wait_recv()

    barrier = pltpu.get_barrier_semaphore()
    partners = [above, below, twin]
    partners += [ring1(lax.rem(pos1 + d, 8)) for d in range(1, 8)]
    partners += [ring2(lax.rem(pos2 + d, 8)) for d in range(1, 8)]
    partners += [across(lax.rem(my_x + d, SIZE_X)) for d in range(1, SIZE_X)]
    for partner in partners:
        pl.semaphore_signal(barrier, inc=1, device_id=partner, device_id_type=MESH)

    down = down_ref[0, 0]
    up = up_ref[0, 0]
    sent = []

    def face(field, slot, plane):
        first, second = widen(field[0, plane]), widen(field[1, plane])
        chosen = jnp.where(slot == 0, first, jnp.where(slot == 1, second, 0.0))
        return chosen.reshape(FACE, LANES).astype(BF16)

    for at, field in enumerate((vox, cot)):
        up_send[at * FACE : (at + 1) * FACE] = face(field, up, EDGE - 1)
        down_send[at * FACE : (at + 1) * FACE] = face(field, down, 0)
    pl.semaphore_wait(barrier, len(partners))
    sent.append(send(up_send, from_lo, halo_s.at[0], halo_r.at[0], above))
    sent.append(send(down_send, from_hi, halo_s.at[1], halo_r.at[1], below))

    def fill(field, wide):
        def body(c, carry):
            planes = pl.ds(lax.rem(c, 2) * CHUNK, CHUNK)
            slot = jnp.where(c < 2, down, up)
            first, second = widen(field[0, planes]), widen(field[1, planes])
            chosen = jnp.where(slot == 0, first, jnp.where(slot == 1, second, 0.0))
            spread(chosen, wide, pl.multiple_of(FACE + c * STEP, FACE))
            return carry

        lax.fori_loop(0, 4, body, 0)

    fill(vox, ax)

    def weights(o, carry):
        rows = pl.ds(pl.multiple_of(o * CH, CH), CH)
        wa[rows] = widen(w1[o]).astype(BF16)
        own = widen(w2[o])
        wb[rows] = own.astype(BF16)
        square = jnp.concatenate([own, jnp.zeros((LANES - CH, LANES), F32)], axis=0)
        wt[pl.ds(pl.multiple_of((26 - o) * CH, CH), CH)] = square.T[:CH].astype(BF16)
        return carry

    lax.fori_loop(0, 27, weights, 0)
    fill(cot, ag)

    def cot_turn(c, carry):
        block = ag[pl.ds(pl.multiple_of(FACE + c * STEP, FACE), STEP), 3 * LANES : 4 * LANES]
        ct[:, pl.ds(pl.multiple_of(c * STEP, STEP), STEP)] = block.astype(F32).T[:CH].astype(BF16)
        return carry

    lax.fori_loop(0, 4, cot_turn, 0)

    def edge_in(buffer, at, valid, wide, row):
        block = buffer[at * FACE : (at + 1) * FACE].astype(F32)
        block = jnp.where(valid, block, 0.0).reshape(1, EDGE, EDGE, LANES)
        spread(block, wide, row)

    lower_valid = space > 0
    upper_valid = space < owners - 1
    last_row = FACE + ROWS
    arrived(from_lo, halo_s.at[0], halo_r.at[0], above)
    edge_in(from_lo, 0, lower_valid, ax, 0)
    edge_in(from_lo, 1, lower_valid, ag, 0)
    arrived(from_hi, halo_s.at[1], halo_r.at[1], below)
    edge_in(from_hi, 0, upper_valid, ax, last_row)
    edge_in(from_hi, 1, upper_valid, ag, last_row)

    def convolve(wide, weight, c):
        total = None
        for i in range(3):
            rows = pl.ds(pl.multiple_of(c * STEP + i * FACE, FACE), STEP)
            product = jnp.dot(
                wide[rows, :WIDE], weight[i * WIDE : (i + 1) * WIDE], preferred_element_type=F32
            )
            total = product if total is None else total + product
        active = jnp.where(c < 2, down, up) < 2
        return total, active

    def first_conv(c):
        total, active = convolve(ax, wa, c)
        before = jnp.where(active, total, 0.0)
        gate = jax.nn.sigmoid(before)
        dslope[pl.ds(pl.multiple_of(c * STEP, STEP), STEP)] = gate * (1.0 + before * (1.0 - gate))
        hidden = (before * gate).astype(BF16).astype(F32)
        spread(
            hidden.reshape(CHUNK, EDGE, EDGE, LANES), ah, pl.multiple_of(FACE + c * STEP, FACE)
        )

    def both_ends(n, carry):
        first_conv(n * 3)
        return carry

    lax.fori_loop(0, 2, both_ends, 0)
    centre = slice(3 * LANES, 4 * LANES)
    hdown_send[...] = ah[FACE : 2 * FACE, centre]
    hup_send[...] = ah[ROWS : ROWS + FACE, centre]
    sent.append(send(hup_send, hfrom_lo, halo_s.at[2], halo_r.at[2], above))
    sent.append(send(hdown_send, hfrom_hi, halo_s.at[3], halo_r.at[3], below))

    def middle(n, carry):
        first_conv(n + 1)
        return carry

    lax.fori_loop(0, 2, middle, 0)

    def through(c, carry):
        total, active = convolve(ag, wt, c)
        rows = pl.ds(pl.multiple_of(c * STEP, STEP), STEP)
        slope = jnp.where(active, total, 0.0) * dslope[rows]
        st[:, rows] = slope.T[:CH].astype(BF16)
        return carry

    lax.fori_loop(0, 4, through, 0)

    def gradient(turned, wide, g):
        def body(i, carry):
            rows = pl.ds(pl.multiple_of(i * FACE, FACE), ROWS)
            block = jnp.dot(turned[...], wide[rows], preferred_element_type=F32)
            for tile in range(TILES_WIDE):
                at = pl.multiple_of((i * TILES_WIDE + tile) * CH, CH)
                part_sum[g, pl.ds(at, CH)] = block[:, LANES * tile : LANES * (tile + 1)]
            return carry

        lax.fori_loop(0, 3, body, 0)
        used = 3 * TILES_WIDE * CH
        part_sum[g, used:] = jnp.zeros((2 * HALF - used, LANES), F32)

    def rows_of(start, count):
        return pl.ds(pl.multiple_of(start, SHARD), count)

    def core_send(g):
        for t in range(8):
            src = part_sum.at[g, rows_of((1 - core) * HALF + t * PART, PART)]
            sent.append(
                send(src, core_in.at[g, pl.ds(t * PART, PART)], s0.at[g, t], r0.at[g, t], twin)
            )

    def core_add(g):
        for t in range(8):
            arrived(core_in.at[g, pl.ds(t * PART, PART)], s0.at[g, t], r0.at[g, t], twin)
        for d in (4, 3, 5, 2, 6, 1, 7, 0):
            t = lax.rem(pos1 + d, 8)
            total = (
                part_sum[g, rows_of(core * HALF + t * PART, PART)]
                + core_in[g, rows_of(t * PART, PART)]
            )
            if d == 0:
                mid[g] = total
            else:
                ring_out[g, d] = total.astype(BF16)
                sent.append(
                    send(ring_out.at[g, d], ring_in.at[g, d], s1.at[g, d], r1.at[g, d], ring1(t))
                )

    def ring1_add(g):
        for d in range(1, 8):
            arrived(ring_in.at[g, d], s1.at[g, d], r1.at[g, d], twin)
        total = mid[g]
        for d in range(1, 8):
            total = total + ring_in[g, d].astype(F32)
        mid[g] = total
        for d in (4, 3, 5, 2, 6, 1, 7):
            t = lax.rem(pos2 + d, 8)
            src = mid.at[g, rows_of(t * SHARD, SHARD)]
            sent.append(send(src, mid_in.at[g, d], s2.at[g, d], r2.at[g, d], ring2(t)))

    def ring2_add(g):
        for d in range(1, 8):
            arrived(mid_in.at[g, d], s2.at[g, d], r2.at[g, d], twin)
        total = mid[g, rows_of(pos2 * SHARD, SHARD)]
        for d in range(1, 8):
            total = total + mid_in[g, d]
        cross[g, my_x] = total
        for d in (2, 1, 3):
            t = lax.rem(my_x + d, SIZE_X)
            sent.append(
                send(cross.at[g, my_x], cross.at[g, my_x], s3.at[g, d], r3.at[g, d], across(t))
            )

    def cross_add(g):
        for d in range(1, SIZE_X):
            t = lax.rem(my_x + SIZE_X - d, SIZE_X)
            arrived(cross.at[g, t], s3.at[g, d], r3.at[g, d], twin)
        total = cross[g, 0]
        for t in range(1, SIZE_X):
            total = total + cross[g, t]
        mine = rows_of(core * HALF + pos1 * PART + pos2 * SHARD, SHARD)
        packed[g, mine] = (total * scale).astype(BF16)
        for d in (4, 3, 5, 2, 6, 1, 7):
            t = lax.rem(pos2 + d, 8)
            sent.append(
                send(packed.at[g, mine], packed.at[g, mine], s4.at[g, d], r4.at[g, d], ring2(t))
            )

    def ring2_gather(g):
        for d in range(1, 8):
            t = lax.rem(pos2 + 8 - d, 8)
            theirs = rows_of(core * HALF + pos1 * PART + t * SHARD, SHARD)
            arrived(packed.at[g, theirs], s4.at[g, d], r4.at[g, d], twin)
        mine = packed.at[g, rows_of(core * HALF + pos1 * PART, PART)]
        for d in (4, 3, 5, 2, 6, 1, 7):
            t = lax.rem(pos1 + d, 8)
            sent.append(send(mine, mine, s5.at[g, d], r5.at[g, d], ring1(t)))
        sent.append(send(mine, mine, s6.at[g, 0], r6.at[g, 0], twin))

    def ring1_gather(g):
        for d in (1, 7, 2, 6, 3, 5, 4):
            t = lax.rem(pos1 + 8 - d, 8)
            theirs = packed.at[g, rows_of(core * HALF + t * PART, PART)]
            arrived(theirs, s5.at[g, d], r5.at[g, d], twin)
            sent.append(send(theirs, theirs, s6.at[g, d], r6.at[g, d], twin))

    def core_gather(g):
        for d in range(8):
            t = lax.rem(pos2 + 8 - d, 8)
            theirs = packed.at[g, rows_of((1 - core) * HALF + t * PART, PART)]
            arrived(theirs, s6.at[g, d], r6.at[g, d], twin)

    gradient(st, ax, 0)
    core_send(0)
    arrived(hfrom_lo, halo_s.at[2], halo_r.at[2], above)
    edge_in(hfrom_lo, 0, lower_valid, ah, 0)
    arrived(hfrom_hi, halo_s.at[3], halo_r.at[3], below)
    edge_in(hfrom_hi, 0, upper_valid, ah, last_row)
    core_add(0)
    gradient(ct, ah, 1)
    core_send(1)
    core_add(1)

    def second_conv(c, carry):
        total, active = convolve(ah, wb, c)
        inputs = ax[pl.ds(pl.multiple_of(FACE + c * STEP, FACE), STEP), centre].astype(F32)
        rows = pl.ds(pl.multiple_of(c * STEP, STEP), STEP)
        sums[rows] = jnp.where(active, total + inputs, 0.0)
        return carry

    lax.fori_loop(0, 4, second_conv, 0)

    def place(n, carry):
        low = sums[pl.ds(pl.multiple_of(n * STEP, STEP), STEP)]
        high = sums[pl.ds(pl.multiple_of(ROWS // 2 + n * STEP, STEP), STEP)]
        for slot in range(2):
            chosen = jnp.where(down == slot, low, jnp.where(up == slot, high, 0.0))
            chosen = chosen.reshape(CHUNK, EDGE, EDGE, LANES)[..., :CH]
            out[slot, pl.ds(n * CHUNK, CHUNK)] = chosen.astype(BF16)
        return carry

    lax.fori_loop(0, 2, place, 0)

    for stage in (ring1_add, ring2_add, cross_add, ring2_gather, ring1_gather, core_gather):
        for g in range(2):
            stage(g)
    for copy in sent:
        copy.wait_send()


def unpack(packed, field, first, second, out):
    out[...] = field[...]
    for g, result in enumerate((first, second)):
        for tile in range(TILES_WIDE):
            turned = packed[g, CH * tile : CH * (tile + 1)].astype(F32).T
            count = min(LANES, WIDE - LANES * tile)
            result[LANES * tile : LANES * tile + count] = turned[:count]


def on_device(voxels, cotangent, weight_first, weight_second, act_count, up_list, down_list, table):
    vmem = pl.BlockSpec(memory_space=pltpu.VMEM)
    smem = pl.BlockSpec(memory_space=pltpu.SMEM)
    scale = 1.0 / math.sqrt(512 * 2 * EDGE**3)
    dma = pltpu.SemaphoreType.DMA
    field_shape = jax.ShapeDtypeStruct((2, EDGE, EDGE, EDGE, CH), BF16)
    packed_shape = jax.ShapeDtypeStruct((2, 2 * HALF, LANES), BF16)
    wide = pltpu.VMEM((ROWS + 2 * FACE, TILES_WIDE * LANES), BF16)
    weight = pltpu.VMEM((27 * CH, LANES), BF16)
    turned = pltpu.VMEM((CH, ROWS), BF16)
    field, packed = pl.pallas_call(
        functools.partial(section, scale),
        out_shape=(field_shape, packed_shape),
        in_specs=[smem, smem, vmem, vmem, vmem, vmem],
        out_specs=(vmem, vmem),
        scratch_shapes=[
            wide, wide, wide, weight, weight, weight,
            pltpu.VMEM((ROWS, LANES), F32),
            pltpu.VMEM((ROWS, LANES), F32),
            turned, turned,
            *[pltpu.VMEM((2 * FACE, LANES), BF16)] * 4,
            *[pltpu.VMEM((FACE, LANES), BF16)] * 4,
            pltpu.VMEM((2, 2 * HALF, LANES), F32),
            pltpu.VMEM((2, HALF, LANES), F32),
            pltpu.VMEM((2, 8, PART, LANES), BF16),
            pltpu.VMEM((2, 8, PART, LANES), BF16),
            pltpu.VMEM((2, PART, LANES), F32),
            pltpu.VMEM((2, 8, SHARD, LANES), F32),
            pltpu.VMEM((2, SIZE_X, SHARD, LANES), F32),
            dma((4,)), dma((4,)),
            *[dma((2, 8))] * 6, *[dma((2, 4))] * 2, *[dma((2, 8))] * 6,
        ],
        compiler_params=pltpu.CompilerParams(
            collective_id=0, has_side_effects=True, vmem_limit_bytes=48 * 2**20
        ),
        name="section",
    )(down_list, up_list, voxels[0], cotangent[0], weight_first, weight_second)
    step_rows = TILES_WIDE * CH
    first, second, out_field = pl.pallas_call(
        unpack,
        grid=(3,),
        out_shape=(jax.ShapeDtypeStruct((27 * CH, CH), F32),) * 2 + (field_shape,),
        in_specs=[
            pl.BlockSpec((2, step_rows, LANES), lambda i: (0, i, 0)),
            pl.BlockSpec(field_shape.shape, lambda i: (0, 0, 0, 0, 0)),
        ],
        out_specs=(
            pl.BlockSpec((WIDE, CH), lambda i: (i, 0)),
            pl.BlockSpec((WIDE, CH), lambda i: (i, 0)),
            pl.BlockSpec(field_shape.shape, lambda i: (0, 0, 0, 0, 0)),
        ),
        compiler_params=pltpu.CompilerParams(vmem_limit_bytes=32 * 2**20),
        name="unpack",
    )(packed, field)
    shape = weight_first.shape
    return (out_field[None], first.reshape(shape), second.reshape(shape))


def solution(mesh):
    in_specs = (
        P("rep", "space", None, None, None, None),
        P("rep", "space", None, None, None, None),
        P(),
        P(),
        P("rep", "space"),
        P("rep", "space"),
        P("rep", "space"),
        P("rep", "space", None),
    )
    out_specs = (P("rep", "space", None, None, None, None), P(), P())
    return jax.shard_map(
        on_device, mesh=mesh, in_specs=in_specs, out_specs=out_specs, check_vma=False
    )
```

```python
import functools
import math

import jax
import jax.numpy as jnp
from jax import lax
from jax.experimental import pallas as pl
from jax.experimental.pallas import tpu as pltpu
from jax.sharding import PartitionSpec as P

F32 = jnp.float32
BF16 = jnp.bfloat16
MESH = pl.DeviceIdType.MESH

SIZE_X, SIZE_Y, SIZE_Z = 4, 8, 8
EDGE = 8
CH = 96
LANES = 128
FACE = EDGE * EDGE
PLANES = 2 * EDGE
ROWS = PLANES * FACE
WIDE = 9 * CH
TILES_WIDE = 7
HALF = 1024
RINGS = ((SIZE_Y, SIZE_Z, SIZE_X), (SIZE_X, SIZE_Y, SIZE_Z))
PART = tuple(HALF // ring[0] for ring in RINGS)
SHARD = tuple(HALF // (ring[0] * ring[1]) for ring in RINGS)
ORDER = {8: (4, 3, 5, 2, 6, 1, 7), 4: (2, 1, 3)}
CHUNK = 4
STEP = CHUNK * FACE


def widen(value):
    value = value.astype(F32)
    blank = jnp.zeros(value.shape[:-1] + (LANES - CH,), F32)
    return jnp.concatenate([value, blank], axis=-1)


def spread(value, out, row):
    planes = value.shape[0]
    flat = value.reshape(planes * EDGE, EDGE, LANES)
    depth = lax.broadcasted_iota(jnp.int32, flat.shape, 1)
    by_depth = [
        jnp.where(depth == 0, 0.0, pltpu.roll(flat, 1, 1)),
        flat,
        jnp.where(depth == EDGE - 1, 0.0, pltpu.roll(flat, EDGE - 1, 1)),
    ]

    def piece(index):
        shift_y, shift_z = index // 3, index % 3
        turned = by_depth[shift_z]
        turn = CH * index % LANES
        if turn:
            turned = pltpu.roll(turned, turn, 2)
        turned = turned.reshape(planes, EDGE, EDGE, LANES)
        blank = jnp.zeros((planes, 1, EDGE, LANES), F32)
        if shift_y == 0:
            turned = jnp.concatenate([blank, turned[:, : EDGE - 1]], axis=1)
        elif shift_y == 2:
            turned = jnp.concatenate([turned[:, 1:], blank], axis=1)
        return turned.reshape(planes * FACE, LANES)

    lane = lax.broadcasted_iota(jnp.int32, (planes * FACE, LANES), 1)
    pieces = [piece(index) for index in range(9)]
    for tile in range(TILES_WIDE):
        first = LANES * tile // CH
        border = CH * (first + 1) - LANES * tile
        block = pieces[first]
        if border < LANES and first + 1 < 9:
            block = jnp.where(lane < border, block, pieces[first + 1])
        out[pl.ds(row, planes * FACE), LANES * tile : LANES * (tile + 1)] = block.astype(BF16)


def section(
    scale,
    down_ref, up_ref, vox_hbm, cot_hbm, w1_hbm, w2_hbm,
    out, packed,
    vox, cot, w1, w2, ax, ah, ag, wt, dslope, sums, st, ct,
    up_send, down_send, from_lo, from_hi, hup_send, hdown_send, hfrom_lo, hfrom_hi,
    part_sum, core_in,
    ring_out0, ring_out1, ring_in0, ring_in1, mid0, mid1, mid_in0, mid_in1, cross0, cross1,
    load_s, halo_s, halo_r, s0, r0, s1, r1, s2, r2, s3, r3, s4, r4, s5, r5, s6, r6,
):
    space = lax.axis_index("space")
    rep = lax.axis_index("rep")
    owners = SIZE_X * SIZE_Z * 2
    y_lo = lax.rem(space, 2)
    my_z = lax.rem(lax.div(space, 2), SIZE_Z)
    my_x = lax.div(space, 2 * SIZE_Z)
    core = lax.rem(rep, 2)
    my_y = lax.div(rep, 2) * 2 + y_lo

    def device(x, y, z, c):
        return ((x * SIZE_Z + z) * 2 + lax.rem(y, 2), lax.div(y, 2) * 2 + c)

    first_yz = (
        my_y * (1 - core) + my_z * core,
        lambda t: device(my_x, t * (1 - core) + my_y * core, my_z * (1 - core) + t * core, core),
    )
    second_yz = (
        my_z * (1 - core) + my_y * core,
        lambda t: device(my_x, my_y * (1 - core) + t * core, t * (1 - core) + my_z * core, core),
    )
    along_x = (my_x, lambda t: device(t, my_y, my_z, core))
    axes = ((first_yz, second_yz, along_x), (along_x, first_yz, second_yz))
    twin_place = (second_yz[0], my_x)

    twin = device(my_x, my_y, my_z, 1 - core)
    above = (lax.rem(space + 1, owners), rep)
    below = (lax.rem(space + owners - 1, owners), rep)

    def send(src, dst, send_sem, recv_sem, target):
        copy = pltpu.make_async_remote_copy(
            src_ref=src, dst_ref=dst, send_sem=send_sem, recv_sem=recv_sem,
            device_id=target, device_id_type=MESH,
        )
        copy.start()
        return copy

    def arrived(dst, send_sem, recv_sem, target):
        pltpu.make_async_remote_copy(
            src_ref=dst, dst_ref=dst, send_sem=send_sem, recv_sem=recv_sem,
            device_id=target, device_id_type=MESH,
        ).wait_recv()

    loads = [
        pltpu.make_async_copy(src, dst, load_s.at[n])
        for n, (src, dst) in enumerate(
            ((vox_hbm, vox), (cot_hbm, cot), (w1_hbm, w1), (w2_hbm, w2))
        )
    ]
    for load in loads:
        load.start()

    barrier = pltpu.get_barrier_semaphore()
    partners = [above, below, twin]
    for (place, at), size in zip(axes[0], RINGS[0]):
        partners += [at(lax.rem(place + d, size)) for d in range(1, size)]
    for partner in partners:
        pl.semaphore_signal(barrier, inc=1, device_id=partner, device_id_type=MESH)

    down = down_ref[0, 0]
    up = up_ref[0, 0]
    sent = []

    def face(field, slot, plane):
        first, second = widen(field[0, plane]), widen(field[1, plane])
        chosen = jnp.where(slot == 0, first, jnp.where(slot == 1, second, 0.0))
        return chosen.reshape(FACE, LANES).astype(BF16)

    loads[0].wait()
    loads[1].wait()
    for at, field in enumerate((vox, cot)):
        up_send[at * FACE : (at + 1) * FACE] = face(field, up, EDGE - 1)
        down_send[at * FACE : (at + 1) * FACE] = face(field, down, 0)
    pl.semaphore_wait(barrier, len(partners))
    sent.append(send(up_send, from_lo, halo_s.at[0], halo_r.at[0], above))
    sent.append(send(down_send, from_hi, halo_s.at[1], halo_r.at[1], below))

    def fill(field, wide):
        def body(c, carry):
            planes = pl.ds(lax.rem(c, 2) * CHUNK, CHUNK)
            slot = jnp.where(c < 2, down, up)
            first, second = widen(field[0, planes]), widen(field[1, planes])
            chosen = jnp.where(slot == 0, first, jnp.where(slot == 1, second, 0.0))
            spread(chosen, wide, pl.multiple_of(FACE + c * STEP, FACE))
            return carry

        lax.fori_loop(0, 4, body, 0, unroll=True)

    fill(vox, ax)

    loads[2].wait()
    loads[3].wait()

    def weights(n, carry):
        for k in range(3):
            o = 3 * n + k
            own = widen(w2[o])
            square = jnp.concatenate([own, jnp.zeros((LANES - CH, LANES), F32)], axis=0)
            wt[26 - o] = square.T[:CH, :CH].astype(BF16)
        return carry

    lax.fori_loop(0, 9, weights, 0, unroll=True)
    fill(cot, ag)

    def cot_turn(c, carry):
        block = ag[pl.ds(pl.multiple_of(FACE + c * STEP, FACE), STEP), 3 * LANES : 4 * LANES]
        ct[:, pl.ds(pl.multiple_of(c * STEP, STEP), STEP)] = block.astype(F32).T[:CH].astype(BF16)
        return carry

    lax.fori_loop(0, 4, cot_turn, 0, unroll=True)

    def edge_in(buffer, at, valid, wide, row):
        block = buffer[at * FACE : (at + 1) * FACE].astype(F32)
        block = jnp.where(valid, block, 0.0).reshape(1, EDGE, EDGE, LANES)
        spread(block, wide, row)

    lower_valid = space > 0
    upper_valid = space < owners - 1
    last_row = FACE + ROWS
    arrived(from_lo, halo_s.at[0], halo_r.at[0], above)
    edge_in(from_lo, 0, lower_valid, ax, 0)
    edge_in(from_lo, 1, lower_valid, ag, 0)
    arrived(from_hi, halo_s.at[1], halo_r.at[1], below)
    edge_in(from_hi, 0, upper_valid, ax, last_row)
    edge_in(from_hi, 1, upper_valid, ag, last_row)

    def convolve(wide, weight, c):
        total = None
        for i in range(3):
            rows = pl.ds(pl.multiple_of(c * STEP + i * FACE, FACE), STEP)
            product = jnp.dot(
                wide[rows, :WIDE],
                weight[9 * i : 9 * i + 9].reshape(WIDE, CH),
                preferred_element_type=F32,
            )
            total = product if total is None else total + product
        total = widen(total)
        active = jnp.where(c < 2, down, up) < 2
        return total, active

    def first_conv(c):
        total, active = convolve(ax, w1, c)
        before = jnp.where(active, total, 0.0)
        gate = jax.nn.sigmoid(before)
        dslope[pl.ds(pl.multiple_of(c * STEP, STEP), STEP)] = gate * (1.0 + before * (1.0 - gate))
        hidden = (before * gate).astype(BF16).astype(F32)
        spread(
            hidden.reshape(CHUNK, EDGE, EDGE, LANES), ah, pl.multiple_of(FACE + c * STEP, FACE)
        )

    def both_ends(n, carry):
        first_conv(n * 3)
        return carry

    lax.fori_loop(0, 2, both_ends, 0, unroll=True)
    centre = slice(3 * LANES, 4 * LANES)
    hdown_send[...] = ah[FACE : 2 * FACE, centre]
    hup_send[...] = ah[ROWS : ROWS + FACE, centre]
    sent.append(send(hup_send, hfrom_lo, halo_s.at[2], halo_r.at[2], above))
    sent.append(send(hdown_send, hfrom_hi, halo_s.at[3], halo_r.at[3], below))

    def middle(n, carry):
        first_conv(n + 1)
        return carry

    lax.fori_loop(0, 2, middle, 0, unroll=True)

    def through(c, carry):
        total, active = convolve(ag, wt, c)
        rows = pl.ds(pl.multiple_of(c * STEP, STEP), STEP)
        slope = jnp.where(active, total, 0.0) * dslope[rows]
        st[:, rows] = slope.T[:CH].astype(BF16)
        return carry

    lax.fori_loop(0, 4, through, 0, unroll=True)

    def gradient(turned, wide, g):
        def body(i, carry):
            rows = pl.ds(pl.multiple_of(i * FACE, FACE), ROWS)
            block = jnp.dot(turned[...], wide[rows], preferred_element_type=F32)
            for tile in range(TILES_WIDE):
                at = pl.multiple_of((i * TILES_WIDE + tile) * CH, CH)
                part_sum[g, pl.ds(at, CH)] = block[:, LANES * tile : LANES * (tile + 1)]
            return carry

        lax.fori_loop(0, 3, body, 0, unroll=True)
        used = 3 * TILES_WIDE * CH
        part_sum[g, used:] = jnp.zeros((2 * HALF - used, LANES), F32)

    ring_out = (ring_out0, ring_out1)
    ring_in = (ring_in0, ring_in1)
    mid = (mid0, mid1)
    mid_in = (mid_in0, mid_in1)
    cross = (cross0, cross1)

    def rows_of(start, count):
        return pl.ds(pl.multiple_of(start, 16), count)

    def core_send(g):
        part = PART[g]
        for t in range(RINGS[g][0]):
            src = part_sum.at[g, rows_of((1 - core) * HALF + t * part, part)]
            dst = core_in.at[g, pl.ds(t * part, part)]
            sent.append(send(src, dst, s0.at[g, t], r0.at[g, t], twin))

    def core_add(g):
        part, size, (place, at) = PART[g], RINGS[g][0], axes[g][0]
        for t in range(size):
            arrived(core_in.at[g, pl.ds(t * part, part)], s0.at[g, t], r0.at[g, t], twin)
        for d in ORDER[size] + (0,):
            t = lax.rem(place + d, size)
            total = (
                part_sum[g, rows_of(core * HALF + t * part, part)]
                + core_in[g, rows_of(t * part, part)]
            )
            if d == 0:
                mid[g][...] = total
            else:
                ring_out[g][d] = total.astype(BF16)
                src, dst = ring_out[g].at[d], ring_in[g].at[d]
                sent.append(send(src, dst, s1.at[g, d], r1.at[g, d], at(t)))

    def ring1_add(g):
        shard, size, (place, at) = SHARD[g], RINGS[g][1], axes[g][1]
        total = mid[g][...]
        for d in range(1, RINGS[g][0]):
            arrived(ring_in[g].at[d], s1.at[g, d], r1.at[g, d], twin)
            total = total + ring_in[g][d].astype(F32)
        mid[g][...] = total
        for d in ORDER[size]:
            t = lax.rem(place + d, size)
            src = mid[g].at[rows_of(t * shard, shard)]
            sent.append(send(src, mid_in[g].at[d], s2.at[g, d], r2.at[g, d], at(t)))

    def ring2_add(g):
        shard, size, (place, at) = SHARD[g], RINGS[g][2], axes[g][2]
        total = mid[g][rows_of(axes[g][1][0] * shard, shard)]
        for d in range(1, RINGS[g][1]):
            arrived(mid_in[g].at[d], s2.at[g, d], r2.at[g, d], twin)
            total = total + mid_in[g][d]
        cross[g][place] = total
        mine = cross[g].at[place]
        for d in ORDER[size]:
            sent.append(send(mine, mine, s3.at[g, d], r3.at[g, d], at(lax.rem(place + d, size))))

    def start_of(g):
        return core * HALF + axes[g][0][0] * PART[g]

    def cross_add(g):
        size, place = RINGS[g][2], axes[g][2][0]
        for d in range(1, size):
            t = lax.rem(place + size - d, size)
            arrived(cross[g].at[t], s3.at[g, d], r3.at[g, d], twin)
        total = cross[g][0]
        for t in range(1, size):
            total = total + cross[g][t]
        shard, size, (place, at) = SHARD[g], RINGS[g][1], axes[g][1]
        rows = rows_of(start_of(g) + place * shard, shard)
        packed[g, rows] = (total * scale).astype(BF16)
        mine = packed.at[g, rows]
        for d in ORDER[size]:
            sent.append(send(mine, mine, s4.at[g, d], r4.at[g, d], at(lax.rem(place + d, size))))

    def ring2_gather(g):
        shard, size, place = SHARD[g], RINGS[g][1], axes[g][1][0]
        for d in range(1, size):
            t = lax.rem(place + size - d, size)
            theirs = packed.at[g, rows_of(start_of(g) + t * shard, shard)]
            arrived(theirs, s4.at[g, d], r4.at[g, d], twin)
        mine = packed.at[g, rows_of(start_of(g), PART[g])]
        size, (place, at) = RINGS[g][0], axes[g][0]
        for d in ORDER[size]:
            sent.append(send(mine, mine, s5.at[g, d], r5.at[g, d], at(lax.rem(place + d, size))))
        sent.append(send(mine, mine, s6.at[g, 0], r6.at[g, 0], twin))

    def ring1_gather(g):
        size, place = RINGS[g][0], axes[g][0][0]
        for d in ORDER[size][::-1]:
            t = lax.rem(place + size - d, size)
            theirs = packed.at[g, rows_of(core * HALF + t * PART[g], PART[g])]
            arrived(theirs, s5.at[g, d], r5.at[g, d], twin)
            sent.append(send(theirs, theirs, s6.at[g, d], r6.at[g, d], twin))

    def core_gather(g):
        size = RINGS[g][0]
        for d in range(size):
            t = lax.rem(twin_place[g] + size - d, size)
            theirs = packed.at[g, rows_of((1 - core) * HALF + t * PART[g], PART[g])]
            arrived(theirs, s6.at[g, d], r6.at[g, d], twin)

    gradient(st, ax, 0)
    core_send(0)
    arrived(hfrom_lo, halo_s.at[2], halo_r.at[2], above)
    edge_in(hfrom_lo, 0, lower_valid, ah, 0)
    arrived(hfrom_hi, halo_s.at[3], halo_r.at[3], below)
    edge_in(hfrom_hi, 0, upper_valid, ah, last_row)
    core_add(0)
    gradient(ct, ah, 1)
    core_send(1)
    core_add(1)

    def second_conv(c, carry):
        total, active = convolve(ah, w2, c)
        inputs = ax[pl.ds(pl.multiple_of(FACE + c * STEP, FACE), STEP), centre].astype(F32)
        rows = pl.ds(pl.multiple_of(c * STEP, STEP), STEP)
        sums[rows] = jnp.where(active, total + inputs, 0.0)
        return carry

    lax.fori_loop(0, 4, second_conv, 0, unroll=True)

    def place(n, carry):
        low = sums[pl.ds(pl.multiple_of(n * STEP, STEP), STEP)]
        high = sums[pl.ds(pl.multiple_of(ROWS // 2 + n * STEP, STEP), STEP)]
        for slot in range(2):
            chosen = jnp.where(down == slot, low, jnp.where(up == slot, high, 0.0))
            chosen = chosen.reshape(CHUNK, EDGE, EDGE, LANES)[..., :CH]
            out[slot, pl.ds(n * CHUNK, CHUNK)] = chosen.astype(BF16)
        return carry

    lax.fori_loop(0, 2, place, 0, unroll=True)

    for stage in (ring1_add, ring2_add, cross_add, ring2_gather, ring1_gather, core_gather):
        for g in range(2):
            stage(g)
    for copy in sent:
        copy.wait_send()


def unpack(packed, field, first, second, out):
    out[...] = field[...]
    for g, result in enumerate((first, second)):
        for tile in range(TILES_WIDE):
            turned = packed[g, CH * tile : CH * (tile + 1)].astype(F32).T
            count = min(LANES, WIDE - LANES * tile)
            result[LANES * tile : LANES * tile + count] = turned[:count]


def on_device(voxels, cotangent, weight_first, weight_second, act_count, up_list, down_list, table):
    vmem = pl.BlockSpec(memory_space=pltpu.VMEM)
    smem = pl.BlockSpec(memory_space=pltpu.SMEM)
    scale = 1.0 / math.sqrt(512 * 2 * EDGE**3)
    dma = pltpu.SemaphoreType.DMA
    field_shape = jax.ShapeDtypeStruct((2, EDGE, EDGE, EDGE, CH), BF16)
    packed_shape = jax.ShapeDtypeStruct((2, 2 * HALF, LANES), BF16)
    wide = pltpu.VMEM((ROWS + 2 * FACE, TILES_WIDE * LANES), BF16)
    weight = pltpu.VMEM((27, CH, CH), BF16)
    bricks = pltpu.VMEM(field_shape.shape, BF16)
    turned = pltpu.VMEM((CH, ROWS), BF16)
    field, packed = pl.pallas_call(
        functools.partial(section, scale),
        out_shape=(field_shape, packed_shape),
        in_specs=[smem, smem] + [pl.BlockSpec(memory_space=pltpu.HBM)] * 4,
        out_specs=(vmem, vmem),
        scratch_shapes=[
            bricks, bricks, weight, weight, wide, wide, wide, weight,
            pltpu.VMEM((ROWS, LANES), F32),
            pltpu.VMEM((ROWS, LANES), F32),
            turned, turned,
            *[pltpu.VMEM((2 * FACE, LANES), BF16)] * 4,
            *[pltpu.VMEM((FACE, LANES), BF16)] * 4,
            pltpu.VMEM((2, 2 * HALF, LANES), F32),
            pltpu.VMEM((2, HALF, LANES), F32),
            *[pltpu.VMEM((ring[0], part, LANES), BF16) for ring, part in zip(RINGS, PART)] * 2,
            *[pltpu.VMEM((part, LANES), F32) for part in PART],
            *[pltpu.VMEM((ring[1], shard, LANES), F32) for ring, shard in zip(RINGS, SHARD)],
            *[pltpu.VMEM((ring[2], shard, LANES), F32) for ring, shard in zip(RINGS, SHARD)],
            dma((4,)),
            dma((4,)), dma((4,)),
            *[dma((2, 8))] * 14,
        ],
        compiler_params=pltpu.CompilerParams(
            collective_id=0, has_side_effects=True, vmem_limit_bytes=48 * 2**20
        ),
        name="section",
    )(down_list, up_list, *[pltpu.with_memory_space_constraint(a, pltpu.HBM) for a in (voxels[0], cotangent[0], weight_first, weight_second)])
    step_rows = TILES_WIDE * CH
    first, second, out_field = pl.pallas_call(
        unpack,
        grid=(3,),
        out_shape=(jax.ShapeDtypeStruct((27 * CH, CH), F32),) * 2 + (field_shape,),
        in_specs=[
            pl.BlockSpec((2, step_rows, LANES), lambda i: (0, i, 0)),
            pl.BlockSpec(field_shape.shape, lambda i: (0, 0, 0, 0, 0)),
        ],
        out_specs=(
            pl.BlockSpec((WIDE, CH), lambda i: (i, 0)),
            pl.BlockSpec((WIDE, CH), lambda i: (i, 0)),
            pl.BlockSpec(field_shape.shape, lambda i: (0, 0, 0, 0, 0)),
        ),
        compiler_params=pltpu.CompilerParams(vmem_limit_bytes=32 * 2**20),
        name="unpack",
    )(packed, field)
    shape = weight_first.shape
    return (out_field[None], first.reshape(shape), second.reshape(shape))


def solution(mesh):
    in_specs = (
        P("rep", "space", None, None, None, None),
        P("rep", "space", None, None, None, None),
        P(),
        P(),
        P("rep", "space"),
        P("rep", "space"),
        P("rep", "space"),
        P("rep", "space", None),
    )
    out_specs = (P("rep", "space", None, None, None, None), P(), P())
    return jax.shard_map(
        on_device, mesh=mesh, in_specs=in_specs, out_specs=out_specs, check_vma=False
    )
```

```python
import functools
import math

import jax
import jax.numpy as jnp
from jax import lax
from jax.experimental import pallas as pl
from jax.experimental.pallas import tpu as pltpu
from jax.sharding import PartitionSpec as P

F32 = jnp.float32
BF16 = jnp.bfloat16
MESH = pl.DeviceIdType.MESH

SIZE_X, SIZE_Y, SIZE_Z = 4, 8, 8
EDGE = 8
CH = 96
LANES = 128
FACE = EDGE * EDGE
PLANES = 2 * EDGE
ROWS = PLANES * FACE
WIDE = 9 * CH
TILES_WIDE = 7
HALF = 1024
GROUP = HALF // SIZE_X
SIDE = 8
SHARD = GROUP // SIDE
STEPS_X = (2, 1, 3, 0)
STEPS = (4, 3, 5, 2, 6, 1, 7)
PLANE = tuple((a, b) for a in STEPS_X for b in STEPS + (0,) if a or b)
AHEAD = 2
CHUNK = 4
STEP = CHUNK * FACE


def widen(value):
    value = value.astype(F32)
    blank = jnp.zeros(value.shape[:-1] + (LANES - CH,), F32)
    return jnp.concatenate([value, blank], axis=-1)


def spread(value, out, row):
    planes = value.shape[0]
    flat = value.reshape(planes * EDGE, EDGE, LANES)
    depth = lax.broadcasted_iota(jnp.int32, flat.shape, 1)
    by_depth = [
        jnp.where(depth == 0, 0.0, pltpu.roll(flat, 1, 1)),
        flat,
        jnp.where(depth == EDGE - 1, 0.0, pltpu.roll(flat, EDGE - 1, 1)),
    ]

    def piece(index):
        shift_y, shift_z = index // 3, index % 3
        turned = by_depth[shift_z]
        turn = CH * index % LANES
        if turn:
            turned = pltpu.roll(turned, turn, 2)
        turned = turned.reshape(planes, EDGE, EDGE, LANES)
        blank = jnp.zeros((planes, 1, EDGE, LANES), F32)
        if shift_y == 0:
            turned = jnp.concatenate([blank, turned[:, : EDGE - 1]], axis=1)
        elif shift_y == 2:
            turned = jnp.concatenate([turned[:, 1:], blank], axis=1)
        return turned.reshape(planes * FACE, LANES)

    lane = lax.broadcasted_iota(jnp.int32, (planes * FACE, LANES), 1)
    pieces = [piece(index) for index in range(9)]
    for tile in range(TILES_WIDE):
        first = LANES * tile // CH
        border = CH * (first + 1) - LANES * tile
        block = pieces[first]
        if border < LANES and first + 1 < 9:
            block = jnp.where(lane < border, block, pieces[first + 1])
        out[pl.ds(row, planes * FACE), LANES * tile : LANES * (tile + 1)] = block.astype(BF16)


def section(
    scale,
    down_ref, up_ref, table, vox_hbm, cot_hbm, w1_hbm, w2_hbm,
    out, packed,
    vox, cot, w1, w2, ax, ah, ag, wt, dslope, sums, st, ct,
    up_send, down_send, from_lo, from_hi,
    part_sum, core_in, plane_out, plane_in, mid, cross,
    load_s, halo_s, halo_r, s0, r0, s1, r1, s2, r2, s3, r3, s4, r4,
):
    space = lax.axis_index("space")
    rep = lax.axis_index("rep")
    owners = SIZE_X * SIZE_Z * 2
    y_lo = lax.rem(space, 2)
    my_z = lax.rem(lax.div(space, 2), SIZE_Z)
    my_x = lax.div(space, 2 * SIZE_Z)
    core = lax.rem(rep, 2)
    my_y = lax.div(rep, 2) * 2 + y_lo

    def device(x, y, z, c):
        return ((x * SIZE_Z + z) * 2 + lax.rem(y, 2), lax.div(y, 2) * 2 + c)

    side = my_z * (1 - core) + my_y * core
    line = my_y * (1 - core) + my_z * core

    def in_plane(x, t):
        return device(x, my_y * (1 - core) + t * core, t * (1 - core) + my_z * core, core)

    def in_line(t):
        return device(my_x, t * (1 - core) + my_y * core, my_z * (1 - core) + t * core, core)

    def moved(a, b):
        return lax.rem(my_x + a, SIZE_X), lax.rem(side + b, SIDE)

    twin = device(my_x, my_y, my_z, 1 - core)
    above = (lax.rem(space + 1, owners), rep)
    below = (lax.rem(space + owners - 1, owners), rep)

    def send(src, dst, send_sem, recv_sem, target):
        copy = pltpu.make_async_remote_copy(
            src_ref=src, dst_ref=dst, send_sem=send_sem, recv_sem=recv_sem,
            device_id=target, device_id_type=MESH,
        )
        copy.start()
        return copy

    def arrived(dst, send_sem, recv_sem, target):
        pltpu.make_async_remote_copy(
            src_ref=dst, dst_ref=dst, send_sem=send_sem, recv_sem=recv_sem,
            device_id=target, device_id_type=MESH,
        ).wait_recv()

    loads = [
        pltpu.make_async_copy(src, dst, load_s.at[n])
        for n, (src, dst) in enumerate(
            ((vox_hbm, vox), (cot_hbm, cot), (w1_hbm, w1), (w2_hbm, w2))
        )
    ]
    for load in loads:
        load.start()

    barrier = pltpu.get_barrier_semaphore()
    partners = [above, below, twin]
    partners += [in_plane(*moved(a, b)) for a, b in PLANE]
    partners += [in_line(lax.rem(line + d, SIDE)) for d in STEPS]
    for partner in partners:
        pl.semaphore_signal(barrier, inc=1, device_id=partner, device_id_type=MESH)

    down = down_ref[0, 0]
    up = up_ref[0, 0]
    sent = []

    def face(field, slot, plane):
        first, second = widen(field[0, plane]), widen(field[1, plane])
        chosen = jnp.where(slot == 0, first, jnp.where(slot == 1, second, 0.0))
        return chosen.reshape(FACE, LANES).astype(BF16)

    loads[0].wait()
    loads[1].wait()
    faces = ((vox, EDGE - 2, 0), (vox, EDGE - 1, 1), (cot, EDGE - 1, 0))
    for at, (field, high, low) in enumerate(faces):
        up_send[at * FACE : (at + 1) * FACE] = face(field, up, high)
        down_send[at * FACE : (at + 1) * FACE] = face(field, down, low)
    pl.semaphore_wait(barrier, len(partners))
    sent.append(send(up_send, from_lo, halo_s.at[0], halo_r.at[0], above))
    sent.append(send(down_send, from_hi, halo_s.at[1], halo_r.at[1], below))

    def fill(field, wide, ahead):
        def body(c, carry):
            planes = pl.ds(lax.rem(c, 2) * CHUNK, CHUNK)
            slot = jnp.where(c < 2, down, up)
            first, second = widen(field[0, planes]), widen(field[1, planes])
            chosen = jnp.where(slot == 0, first, jnp.where(slot == 1, second, 0.0))
            spread(chosen, wide, pl.multiple_of(ahead * FACE + c * STEP, FACE))
            return carry

        lax.fori_loop(0, 4, body, 0, unroll=True)

    fill(vox, ax, AHEAD)

    loads[2].wait()
    loads[3].wait()

    def weights(n, carry):
        for k in range(3):
            o = 3 * n + k
            own = widen(w2[o])
            square = jnp.concatenate([own, jnp.zeros((LANES - CH, LANES), F32)], axis=0)
            wt[26 - o] = square.T[:CH, :CH].astype(BF16)
        return carry

    lax.fori_loop(0, 9, weights, 0, unroll=True)
    fill(cot, ag, 1)

    def cot_turn(c, carry):
        block = ag[pl.ds(pl.multiple_of(FACE + c * STEP, FACE), STEP), 3 * LANES : 4 * LANES]
        ct[:, pl.ds(pl.multiple_of(c * STEP, STEP), STEP)] = block.astype(F32).T[:CH].astype(BF16)
        return carry

    lax.fori_loop(0, 4, cot_turn, 0, unroll=True)

    def linked(slot, way):
        entry = jnp.where(slot == 0, table[0, 0, way], jnp.where(slot == 1, table[0, 1, way], 3))
        return entry == 2

    lower_active, upper_active = linked(down, 1), linked(up, 7)

    def keep(value, planes):
        kept = []
        for k, plane in enumerate(planes):
            if plane < 0:
                active = lower_active
            elif plane >= PLANES:
                active = upper_active
            else:
                active = (down if plane < EDGE else up) < 2
            kept.append(jnp.where(active, value[k * FACE : (k + 1) * FACE], 0.0))
        return jnp.concatenate(kept, axis=0)

    def runs(planes):
        found = []
        for k, plane in enumerate(planes):
            if k and plane == planes[k - 1] + 1:
                found[-1][2] += 1
            else:
                found.append([k, plane, 1])
        return found

    def convolve(wide, weight, planes, ahead):
        total = None
        for i in range(3):
            rows = [
                wide[(first + ahead - 1 + i) * FACE : (first + ahead - 1 + i + count) * FACE, :WIDE]
                for _, first, count in runs(planes)
            ]
            product = jnp.dot(
                rows[0] if len(rows) == 1 else jnp.concatenate(rows, axis=0),
                weight[9 * i : 9 * i + 9].reshape(WIDE, CH),
                preferred_element_type=F32,
            )
            total = product if total is None else total + product
        return widen(total)

    def first_conv(planes):
        before = keep(convolve(ax, w1, planes, AHEAD), planes)
        gate = jax.nn.sigmoid(before)
        factor = gate * (1.0 + before * (1.0 - gate))
        hidden = (before * gate).astype(BF16).astype(F32)
        for k, plane in enumerate(planes):
            if 0 <= plane < PLANES:
                dslope[plane * FACE : (plane + 1) * FACE] = factor[k * FACE : (k + 1) * FACE]
        for k, first, count in runs(planes):
            block = hidden[k * FACE : (k + count) * FACE].reshape(count, EDGE, EDGE, LANES)
            spread(block, ah, (first + 1) * FACE)

    def through(planes):
        total = keep(convolve(ag, wt, planes, 1), planes)
        for k, first, count in runs(planes):
            rows = slice(first * FACE, (first + count) * FACE)
            slope = total[k * FACE : (k + count) * FACE] * dslope[rows]
            st[:, rows] = slope.T[:CH].astype(BF16)

    inner = ((2, 3, 4, 5), (6, 7, 8, 9), (10, 11, 12, 13))
    for planes in inner:
        first_conv(planes)
    for planes in inner:
        through(planes)

    def edge_in(buffer, at, count, valid, wide, row):
        block = buffer[at * FACE : (at + count) * FACE].astype(F32)
        block = jnp.where(valid, block, 0.0).reshape(count, EDGE, EDGE, LANES)
        spread(block, wide, row)

    lower_valid = space > 0
    upper_valid = space < owners - 1
    arrived(from_lo, halo_s.at[0], halo_r.at[0], above)
    edge_in(from_lo, 0, AHEAD, lower_valid, ax, 0)
    edge_in(from_lo, AHEAD, 1, lower_valid, ag, 0)
    arrived(from_hi, halo_s.at[1], halo_r.at[1], below)
    edge_in(from_hi, 0, AHEAD, upper_valid, ax, (PLANES + AHEAD) * FACE)
    edge_in(from_hi, AHEAD, 1, upper_valid, ag, (PLANES + 1) * FACE)
    first_conv((-1, 0, 1, 14, 15, 16))
    through((0, 1, 14, 15))
    centre = slice(3 * LANES, 4 * LANES)

    def gradient(turned, wide, g, ahead, k):
        i = k * core + (2 - k) * (1 - core)
        rows = pl.ds(pl.multiple_of((i + ahead - 1) * FACE, FACE), ROWS)
        block = jnp.dot(turned[...], wide[rows], preferred_element_type=F32)
        for tile in range(TILES_WIDE):
            at = pl.multiple_of((i * TILES_WIDE + tile) * CH, CH)
            part_sum[g, pl.ds(at, CH)] = block[:, LANES * tile : LANES * (tile + 1)]

    def rows_of(start, count):
        return pl.ds(pl.multiple_of(start, SHARD), count)

    def core_send(g):
        for a in STEPS_X:
            start = lax.rem(my_x + a, SIZE_X) * GROUP
            src = part_sum.at[g, rows_of((1 - core) * HALF + start, GROUP)]
            dst = core_in.at[g, rows_of(start, GROUP)]
            sent.append(send(src, dst, s0.at[g, a], r0.at[g, a], twin))

    def core_add(g):
        for a in STEPS_X:
            start = lax.rem(my_x + a, SIZE_X) * GROUP
            arrived(core_in.at[g, rows_of(start, GROUP)], s0.at[g, a], r0.at[g, a], twin)
            for b in STEPS + (0,):
                x, t = moved(a, b)
                at = x * GROUP + t * SHARD
                total = part_sum[g, rows_of(core * HALF + at, SHARD)] + core_in[g, rows_of(at, SHARD)]
                if (a, b) == (0, 0):
                    mid[g] = total
                else:
                    n = a * SIDE + b
                    plane_out[g, n] = total.astype(BF16)
                    src, dst = plane_out.at[g, n], plane_in.at[g, n]
                    sent.append(send(src, dst, s1.at[g, n], r1.at[g, n], in_plane(x, t)))

    def plane_add(g):
        total = mid[g]
        for a, b in PLANE[::-1]:
            n = a * SIDE + b
            arrived(plane_in.at[g, n], s1.at[g, n], r1.at[g, n], twin)
            total = total + plane_in[g, n].astype(F32)
        cross[g, line] = total
        mine = cross.at[g, line]
        for d in STEPS:
            target = in_line(lax.rem(line + d, SIDE))
            sent.append(send(mine, mine, s2.at[g, d], r2.at[g, d], target))

    def place_of(x, t):
        return rows_of(core * HALF + x * GROUP + t * SHARD, SHARD)

    def line_add(g):
        for d in STEPS[::-1]:
            theirs = cross.at[g, lax.rem(line + SIDE - d, SIDE)]
            arrived(theirs, s2.at[g, d], r2.at[g, d], twin)
        total = cross[g, 0]
        for t in range(1, SIDE):
            total = total + cross[g, t]
        packed[g, place_of(my_x, side)] = (total * scale).astype(BF16)
        mine = packed.at[g, place_of(my_x, side)]
        for a, b in PLANE:
            n = a * SIDE + b
            sent.append(send(mine, mine, s3.at[g, n], r3.at[g, n], in_plane(*moved(a, b))))

    def plane_gather(g):
        for a in STEPS_X[::-1]:
            x = lax.rem(my_x + SIZE_X - a, SIZE_X)
            for b in (0,) + STEPS[::-1]:
                if (a, b) != (0, 0):
                    n = a * SIDE + b
                    theirs = packed.at[g, place_of(x, lax.rem(side + SIDE - b, SIDE))]
                    arrived(theirs, s3.at[g, n], r3.at[g, n], twin)
            group = packed.at[g, rows_of(core * HALF + x * GROUP, GROUP)]
            sent.append(send(group, group, s4.at[g, a], r4.at[g, a], twin))

    def core_gather(g):
        for a in STEPS_X[::-1]:
            x = lax.rem(my_x + SIZE_X - a, SIZE_X)
            group = packed.at[g, rows_of((1 - core) * HALF + x * GROUP, GROUP)]
            arrived(group, s4.at[g, a], r4.at[g, a], twin)

    used = 3 * TILES_WIDE * CH
    for g in range(2):
        part_sum[g, used:] = jnp.zeros((2 * HALF - used, LANES), F32)
    gradient(st, ax, 0, AHEAD, 0)
    gradient(st, ax, 0, AHEAD, 1)
    core_send(0)
    gradient(st, ax, 0, AHEAD, 2)
    gradient(ct, ah, 1, 1, 0)
    gradient(ct, ah, 1, 1, 1)
    core_send(1)
    core_add(0)
    gradient(ct, ah, 1, 1, 2)
    core_add(1)

    for planes in ((0, 1, 2, 3), (4, 5, 6, 7), (8, 9, 10, 11), (12, 13, 14, 15)):
        first, count = planes[0], len(planes)
        total = convolve(ah, w2, planes, 1)
        inputs = ax[(first + AHEAD) * FACE : (first + AHEAD + count) * FACE, centre].astype(F32)
        sums[first * FACE : (first + count) * FACE] = keep(total + inputs, planes)

    def place(n, carry):
        low = sums[pl.ds(pl.multiple_of(n * STEP, STEP), STEP)]
        high = sums[pl.ds(pl.multiple_of(ROWS // 2 + n * STEP, STEP), STEP)]
        for slot in range(2):
            chosen = jnp.where(down == slot, low, jnp.where(up == slot, high, 0.0))
            chosen = chosen.reshape(CHUNK, EDGE, EDGE, LANES)[..., :CH]
            out[slot, pl.ds(n * CHUNK, CHUNK)] = chosen.astype(BF16)
        return carry

    lax.fori_loop(0, 2, place, 0, unroll=True)

    for stage in (plane_add, line_add, plane_gather, core_gather):
        for g in range(2):
            stage(g)
    for copy in sent:
        copy.wait_send()


def unpack(packed, field, first, second, out):
    out[...] = field[...]
    for g, result in enumerate((first, second)):
        for tile in range(TILES_WIDE):
            turned = packed[g, CH * tile : CH * (tile + 1)].astype(F32).T
            count = min(LANES, WIDE - LANES * tile)
            result[LANES * tile : LANES * tile + count] = turned[:count]


def on_device(voxels, cotangent, weight_first, weight_second, act_count, up_list, down_list, table):
    vmem = pl.BlockSpec(memory_space=pltpu.VMEM)
    smem = pl.BlockSpec(memory_space=pltpu.SMEM)
    scale = 1.0 / math.sqrt(512 * 2 * EDGE**3)
    dma = pltpu.SemaphoreType.DMA
    field_shape = jax.ShapeDtypeStruct((2, EDGE, EDGE, EDGE, CH), BF16)
    packed_shape = jax.ShapeDtypeStruct((2, 2 * HALF, LANES), BF16)
    wide = pltpu.VMEM((ROWS + 2 * FACE, TILES_WIDE * LANES), BF16)
    wider = pltpu.VMEM((ROWS + 2 * AHEAD * FACE, TILES_WIDE * LANES), BF16)
    weight = pltpu.VMEM((27, CH, CH), BF16)
    bricks = pltpu.VMEM(field_shape.shape, BF16)
    turned = pltpu.VMEM((CH, ROWS), BF16)
    field, packed = pl.pallas_call(
        functools.partial(section, scale),
        out_shape=(field_shape, packed_shape),
        in_specs=[smem, smem, smem] + [pl.BlockSpec(memory_space=pltpu.HBM)] * 4,
        out_specs=(vmem, vmem),
        scratch_shapes=[
            bricks, bricks, weight, weight, wider, wide, wide, weight,
            pltpu.VMEM((ROWS, LANES), F32),
            pltpu.VMEM((ROWS, LANES), F32),
            turned, turned,
            *[pltpu.VMEM(((AHEAD + 1) * FACE, LANES), BF16)] * 4,
            pltpu.VMEM((2, 2 * HALF, LANES), F32),
            pltpu.VMEM((2, HALF, LANES), F32),
            pltpu.VMEM((2, SIZE_X * SIDE, SHARD, LANES), BF16),
            pltpu.VMEM((2, SIZE_X * SIDE, SHARD, LANES), BF16),
            pltpu.VMEM((2, SHARD, LANES), F32),
            pltpu.VMEM((2, SIDE, SHARD, LANES), F32),
            dma((4,)), dma((2,)), dma((2,)),
            *[dma((2, SIZE_X))] * 2, *[dma((2, SIZE_X * SIDE))] * 2,
            *[dma((2, SIDE))] * 2, *[dma((2, SIZE_X * SIDE))] * 2, *[dma((2, SIZE_X))] * 2,
        ],
        compiler_params=pltpu.CompilerParams(
            collective_id=0, has_side_effects=True, vmem_limit_bytes=48 * 2**20
        ),
        name="section",
    )(
        down_list, up_list, table,
        *[
            pltpu.with_memory_space_constraint(array, pltpu.HBM)
            for array in (voxels[0], cotangent[0], weight_first, weight_second)
        ],
    )
    step_rows = TILES_WIDE * CH
    first, second, out_field = pl.pallas_call(
        unpack,
        grid=(3,),
        out_shape=(jax.ShapeDtypeStruct((27 * CH, CH), F32),) * 2 + (field_shape,),
        in_specs=[
            pl.BlockSpec((2, step_rows, LANES), lambda i: (0, i, 0)),
            pl.BlockSpec(field_shape.shape, lambda i: (0, 0, 0, 0, 0)),
        ],
        out_specs=(
            pl.BlockSpec((WIDE, CH), lambda i: (i, 0)),
            pl.BlockSpec((WIDE, CH), lambda i: (i, 0)),
            pl.BlockSpec(field_shape.shape, lambda i: (0, 0, 0, 0, 0)),
        ),
        compiler_params=pltpu.CompilerParams(vmem_limit_bytes=32 * 2**20),
        name="unpack",
    )(packed, field)
    shape = weight_first.shape
    return (out_field[None], first.reshape(shape), second.reshape(shape))


def solution(mesh):
    in_specs = (
        P("rep", "space", None, None, None, None),
        P("rep", "space", None, None, None, None),
        P(),
        P(),
        P("rep", "space"),
        P("rep", "space"),
        P("rep", "space"),
        P("rep", "space", None),
    )
    out_specs = (P("rep", "space", None, None, None, None), P(), P())
    return jax.shard_map(
        on_device, mesh=mesh, in_specs=in_specs, out_specs=out_specs, check_vma=False
    )
```

```python
import functools
import math

import jax
import jax.numpy as jnp
from jax import lax
from jax.experimental import pallas as pl
from jax.experimental.pallas import tpu as pltpu
from jax.sharding import PartitionSpec as P

F32 = jnp.float32
BF16 = jnp.bfloat16
MESH = pl.DeviceIdType.MESH

SIZE_X, SIZE_Y, SIZE_Z = 4, 8, 8
EDGE = 8
CH = 96
LANES = 128
FACE = EDGE * EDGE
PLANES = 2 * EDGE
ROWS = PLANES * FACE
WIDE = 9 * CH
TILES_WIDE = 7
HALF = 1024
GROUP = HALF // SIZE_X
SIDE = 8
SHARD = GROUP // SIDE
STEPS_X = (2, 1, 3, 0)
STEPS = (4, 3, 5, 2, 6, 1, 7)
PLANE = tuple((a, b) for a in STEPS_X for b in STEPS + (0,) if a or b)
FLAG_ROWS = 16
AHEAD = 2
CHUNK = 4
STEP = CHUNK * FACE


def widen(value):
    value = value.astype(F32)
    blank = jnp.zeros(value.shape[:-1] + (LANES - CH,), F32)
    return jnp.concatenate([value, blank], axis=-1)


def spread(value, out, row):
    planes = value.shape[0]
    flat = value.reshape(planes * EDGE, EDGE, LANES)
    depth = lax.broadcasted_iota(jnp.int32, flat.shape, 1)
    by_depth = [
        jnp.where(depth == 0, 0.0, pltpu.roll(flat, 1, 1)),
        flat,
        jnp.where(depth == EDGE - 1, 0.0, pltpu.roll(flat, EDGE - 1, 1)),
    ]

    def piece(index):
        shift_y, shift_z = index // 3, index % 3
        turned = by_depth[shift_z]
        turn = CH * index % LANES
        if turn:
            turned = pltpu.roll(turned, turn, 2)
        turned = turned.reshape(planes, EDGE, EDGE, LANES)
        blank = jnp.zeros((planes, 1, EDGE, LANES), F32)
        if shift_y == 0:
            turned = jnp.concatenate([blank, turned[:, : EDGE - 1]], axis=1)
        elif shift_y == 2:
            turned = jnp.concatenate([turned[:, 1:], blank], axis=1)
        return turned.reshape(planes * FACE, LANES)

    lane = lax.broadcasted_iota(jnp.int32, (planes * FACE, LANES), 1)
    pieces = [piece(index) for index in range(9)]
    for tile in range(TILES_WIDE):
        first = LANES * tile // CH
        border = CH * (first + 1) - LANES * tile
        block = pieces[first]
        if border < LANES and first + 1 < 9:
            block = jnp.where(lane < border, block, pieces[first + 1])
        out[pl.ds(row, planes * FACE), LANES * tile : LANES * (tile + 1)] = block.astype(BF16)


def section(
    scale,
    down_ref, up_ref, vox_hbm, cot_hbm, w1_hbm, w2_hbm,
    out, packed,
    vox, cot, w1, w2, ax, ah, ag, wt, dslope, slopes, sums, st, ct,
    up_send, down_send, from_lo, from_hi,
    part_sum, core_in, plane_out, plane_in, mid, cross,
    load_s, halo_s, halo_r, s0, r0, s1, r1, s2, r2, s3, r3, s4, r4,
):
    space = lax.axis_index("space")
    rep = lax.axis_index("rep")
    owners = SIZE_X * SIZE_Z * 2
    y_lo = lax.rem(space, 2)
    my_z = lax.rem(lax.div(space, 2), SIZE_Z)
    my_x = lax.div(space, 2 * SIZE_Z)
    core = lax.rem(rep, 2)
    my_y = lax.div(rep, 2) * 2 + y_lo

    def device(x, y, z, c):
        return ((x * SIZE_Z + z) * 2 + lax.rem(y, 2), lax.div(y, 2) * 2 + c)

    side = my_z * (1 - core) + my_y * core
    line = my_y * (1 - core) + my_z * core

    def in_plane(x, t):
        return device(x, my_y * (1 - core) + t * core, t * (1 - core) + my_z * core, core)

    def in_line(t):
        return device(my_x, t * (1 - core) + my_y * core, my_z * (1 - core) + t * core, core)

    def moved(a, b):
        return lax.rem(my_x + a, SIZE_X), lax.rem(side + b, SIDE)

    twin = device(my_x, my_y, my_z, 1 - core)
    above = (lax.rem(space + 1, owners), rep)
    below = (lax.rem(space + owners - 1, owners), rep)

    def send(src, dst, send_sem, recv_sem, target):
        copy = pltpu.make_async_remote_copy(
            src_ref=src, dst_ref=dst, send_sem=send_sem, recv_sem=recv_sem,
            device_id=target, device_id_type=MESH,
        )
        copy.start()
        return copy

    def arrived(dst, send_sem, recv_sem, target):
        pltpu.make_async_remote_copy(
            src_ref=dst, dst_ref=dst, send_sem=send_sem, recv_sem=recv_sem,
            device_id=target, device_id_type=MESH,
        ).wait_recv()

    loads = [
        pltpu.make_async_copy(src, dst, load_s.at[n])
        for n, (src, dst) in enumerate(
            ((vox_hbm, vox), (cot_hbm, cot), (w1_hbm, w1), (w2_hbm, w2))
        )
    ]
    for load in loads:
        load.start()

    barrier = pltpu.get_barrier_semaphore()
    partners = [above, below, twin]
    partners += [in_plane(*moved(a, b)) for a, b in PLANE]
    partners += [in_line(lax.rem(line + d, SIDE)) for d in STEPS]
    for partner in partners:
        pl.semaphore_signal(barrier, inc=1, device_id=partner, device_id_type=MESH)

    down = down_ref[0, 0]
    up = up_ref[0, 0]
    sent = []

    def face(field, slot, plane):
        first, second = widen(field[0, plane]), widen(field[1, plane])
        chosen = jnp.where(slot == 0, first, jnp.where(slot == 1, second, 0.0))
        return chosen.reshape(FACE, LANES).astype(BF16)

    loads[0].wait()
    loads[1].wait()
    faces = ((vox, EDGE - 2, 0), (vox, EDGE - 1, 1), (cot, EDGE - 1, 0))
    for at, (field, high, low) in enumerate(faces):
        up_send[at * FACE : (at + 1) * FACE] = face(field, up, high)
        down_send[at * FACE : (at + 1) * FACE] = face(field, down, low)
    flags = (AHEAD + 1) * FACE
    for buffer, slot in ((up_send, up), (down_send, down)):
        buffer[flags:] = jnp.where(slot < 2, 1.0, 0.0) * jnp.ones((FLAG_ROWS, LANES), BF16)
    pl.semaphore_wait(barrier, len(partners))
    sent.append(send(up_send, from_lo, halo_s.at[0], halo_r.at[0], above))
    sent.append(send(down_send, from_hi, halo_s.at[1], halo_r.at[1], below))

    def fill(field, wide, ahead):
        def body(c, carry):
            planes = pl.ds(lax.rem(c, 2) * CHUNK, CHUNK)
            slot = jnp.where(c < 2, down, up)
            first, second = widen(field[0, planes]), widen(field[1, planes])
            chosen = jnp.where(slot == 0, first, jnp.where(slot == 1, second, 0.0))
            spread(chosen, wide, pl.multiple_of(ahead * FACE + c * STEP, FACE))
            return carry

        lax.fori_loop(0, 4, body, 0, unroll=True)

    def weights(n, carry):
        for k in range(3):
            o = 3 * n + k
            own = widen(w2[o])
            square = jnp.concatenate([own, jnp.zeros((LANES - CH, LANES), F32)], axis=0)
            wt[26 - o] = square.T[:CH, :CH].astype(BF16)
        return carry

    lower_valid = space > 0
    upper_valid = space < owners - 1

    def cot_turn(c, carry):
        block = ag[pl.ds(pl.multiple_of(FACE + c * STEP, FACE), STEP), 3 * LANES : 4 * LANES]
        ct[:, pl.ds(pl.multiple_of(c * STEP, STEP), STEP)] = block.astype(F32).T[:CH].astype(BF16)
        return carry

    def neighbour(buffer, valid):
        flag = buffer[flags : flags + FLAG_ROWS].astype(F32)[:1]
        return jnp.where(valid, flag, 0.0) > 0.5

    def keep(value, planes):
        kept = []
        for k, plane in enumerate(planes):
            if plane < 0:
                active = neighbour(from_lo, lower_valid)
            elif plane >= PLANES:
                active = neighbour(from_hi, upper_valid)
            else:
                active = (down if plane < EDGE else up) < 2
            kept.append(jnp.where(active, value[k * FACE : (k + 1) * FACE], 0.0))
        return jnp.concatenate(kept, axis=0)

    def runs(planes):
        found = []
        for k, plane in enumerate(planes):
            if k and plane == planes[k - 1] + 1:
                found[-1][2] += 1
            else:
                found.append([k, plane, 1])
        return found

    def convolve(wide, weight, planes, ahead):
        total = None
        for i in range(3):
            rows = [
                wide[(first + ahead - 1 + i) * FACE : (first + ahead - 1 + i + count) * FACE, :WIDE]
                for _, first, count in runs(planes)
            ]
            product = jnp.dot(
                rows[0] if len(rows) == 1 else jnp.concatenate(rows, axis=0),
                weight[9 * i : 9 * i + 9].reshape(WIDE, CH),
                preferred_element_type=F32,
            )
            total = product if total is None else total + product
        return widen(total)

    def first_conv(planes):
        before = keep(convolve(ax, w1, planes, AHEAD), planes)
        gate = jax.nn.sigmoid(before)
        factor = gate * (1.0 + before * (1.0 - gate))
        hidden = (before * gate).astype(BF16).astype(F32)
        for k, plane in enumerate(planes):
            if 0 <= plane < PLANES:
                dslope[plane * FACE : (plane + 1) * FACE] = factor[k * FACE : (k + 1) * FACE]
        for k, first, count in runs(planes):
            block = hidden[k * FACE : (k + count) * FACE].reshape(count, EDGE, EDGE, LANES)
            spread(block, ah, (first + 1) * FACE)

    def through(planes):
        total = keep(convolve(ag, wt, planes, 1), planes)
        for k, first, count in runs(planes):
            rows = slice(first * FACE, (first + count) * FACE)
            slopes[rows] = total[k * FACE : (k + count) * FACE] * dslope[rows]

    def turn(pairs):
        for pair in pairs:
            rows = slice(pair * 2 * FACE, (pair + 1) * 2 * FACE)
            st[:, rows] = slopes[rows].T[:CH].astype(BF16)

    def gradient(turned, wide, g, ahead, k, inside):
        i = k * core + (2 - k) * (1 - core)

        def rows(plane, count):
            return pl.ds(pl.multiple_of((i + ahead - 1 + plane) * FACE, FACE), count * FACE)

        if inside:
            left, right = turned[:, 2 * FACE : 14 * FACE], wide[rows(2, 12)]
        else:
            left = jnp.concatenate([turned[:, : 2 * FACE], turned[:, 14 * FACE :]], axis=1)
            right = jnp.concatenate([wide[rows(0, 2)], wide[rows(14, 2)]], axis=0)
        block = jnp.dot(left, right, preferred_element_type=F32)
        for tile in range(TILES_WIDE):
            at = pl.ds(pl.multiple_of((i * TILES_WIDE + tile) * CH, CH), CH)
            part = block[:, LANES * tile : LANES * (tile + 1)]
            part_sum[g, at] = part if inside else part_sum[g, at] + part

    fill(vox, ax, AHEAD)
    inner = ((1, 2, 3, 4), (5, 6, 7), (8, 9, 10), (11, 12, 13, 14))
    loads[2].wait()
    for planes in inner:
        first_conv(planes)
    loads[3].wait()
    lax.fori_loop(0, 9, weights, 0, unroll=True)
    fill(cot, ag, 1)
    lax.fori_loop(0, 4, cot_turn, 0, unroll=True)
    for planes in inner:
        through(planes)
    turn(range(1, 7))
    used = 3 * TILES_WIDE * CH
    for g in range(2):
        part_sum[g, used:] = jnp.zeros((2 * HALF - used, LANES), F32)
    for k in range(3):
        gradient(st, ax, 0, AHEAD, k, True)
    for k in range(3):
        gradient(ct, ah, 1, 1, k, True)

    def edge_in(buffer, at, count, valid, wide, row):
        block = buffer[at * FACE : (at + count) * FACE].astype(F32)
        block = jnp.where(valid, block, 0.0).reshape(count, EDGE, EDGE, LANES)
        spread(block, wide, row)

    arrived(from_lo, halo_s.at[0], halo_r.at[0], above)
    arrived(from_hi, halo_s.at[1], halo_r.at[1], below)
    edge_in(from_lo, 0, AHEAD, lower_valid, ax, 0)
    edge_in(from_hi, 0, AHEAD, upper_valid, ax, (PLANES + AHEAD) * FACE)
    first_conv((-1, 0, 15, 16))
    edge_in(from_lo, AHEAD, 1, lower_valid, ag, 0)
    edge_in(from_hi, AHEAD, 1, upper_valid, ag, (PLANES + 1) * FACE)
    through((0, 15))
    turn((0, 7))
    centre = slice(3 * LANES, 4 * LANES)

    def rows_of(start, count):
        return pl.ds(pl.multiple_of(start, SHARD), count)

    def other(k, me):
        return k + jnp.where(k >= me, 1, 0)

    def core_send(g):
        for a in STEPS_X:
            start = lax.rem(my_x + a, SIZE_X) * GROUP
            src = part_sum.at[g, rows_of((1 - core) * HALF + start, GROUP)]
            dst = core_in.at[g, rows_of(start, GROUP)]
            sent.append(send(src, dst, s0.at[g, a], r0.at[g, a], twin))

    def core_add(g):
        for a in STEPS_X:
            start = lax.rem(my_x + a, SIZE_X) * GROUP
            arrived(core_in.at[g, rows_of(start, GROUP)], s0.at[g, a], r0.at[g, a], twin)
            for b in STEPS + (0,):
                x, t = moved(a, b)
                at = x * GROUP + t * SHARD
                total = part_sum[g, rows_of(core * HALF + at, SHARD)] + core_in[g, rows_of(at, SHARD)]
                if (a, b) == (0, 0):
                    mid[g] = total
                else:
                    n = a * SIDE + b
                    plane_out[g, n] = total.astype(BF16)
                    src, dst = plane_out.at[g, n], plane_in.at[g, n]
                    sent.append(send(src, dst, s1.at[g, n], r1.at[g, n], in_plane(x, t)))

    def plane_add(g):
        total = mid[g]
        for a, b in PLANE[::-1]:
            n = a * SIDE + b
            arrived(plane_in.at[g, n], s1.at[g, n], r1.at[g, n], twin)
            total = total + plane_in[g, n].astype(F32)
        cross[g, line] = total
        mine = cross.at[g, line]
        for k in range(SIDE - 1):
            target = in_line(other(k, line))
            sent.append(send(mine, mine, s2.at[g, k], r2.at[g, line], target))

    def place_of(x, t):
        return rows_of(core * HALF + x * GROUP + t * SHARD, SHARD)

    def line_add(g):
        for d in STEPS[::-1]:
            t = lax.rem(line + SIDE - d, SIDE)
            arrived(cross.at[g, t], s2.at[g, d], r2.at[g, t], twin)
        total = cross[g, 0]
        for t in range(1, SIDE):
            total = total + cross[g, t]
        packed[g, place_of(my_x, side)] = (total * scale).astype(BF16)
        mine = packed.at[g, place_of(my_x, side)]
        me = side * SIZE_X + my_x
        for k in range(SIDE * SIZE_X - 1):
            at = other(k, me)
            target = in_plane(lax.rem(at, SIZE_X), lax.div(at, SIZE_X))
            sent.append(send(mine, mine, s3.at[g, k], r3.at[g, me], target))

    def plane_gather(g):
        for a in STEPS_X[::-1]:
            x = lax.rem(my_x + SIZE_X - a, SIZE_X)
            for b in (0,) + STEPS[::-1]:
                if (a, b) != (0, 0):
                    t = lax.rem(side + SIDE - b, SIDE)
                    theirs = packed.at[g, place_of(x, t)]
                    arrived(theirs, s3.at[g, 0], r3.at[g, t * SIZE_X + x], twin)
            group = packed.at[g, rows_of(core * HALF + x * GROUP, GROUP)]
            sent.append(send(group, group, s4.at[g, a], r4.at[g, a], twin))

    def core_gather(g):
        for a in STEPS_X[::-1]:
            x = lax.rem(my_x + SIZE_X - a, SIZE_X)
            group = packed.at[g, rows_of((1 - core) * HALF + x * GROUP, GROUP)]
            arrived(group, s4.at[g, a], r4.at[g, a], twin)

    gradient(st, ax, 0, AHEAD, 0, False)
    gradient(st, ax, 0, AHEAD, 1, False)
    core_send(0)
    gradient(st, ax, 0, AHEAD, 2, False)
    gradient(ct, ah, 1, 1, 0, False)
    gradient(ct, ah, 1, 1, 1, False)
    core_send(1)
    core_add(0)
    gradient(ct, ah, 1, 1, 2, False)
    core_add(1)

    for planes in ((0, 1, 2, 3), (4, 5, 6, 7), (8, 9, 10, 11), (12, 13, 14, 15)):
        first, count = planes[0], len(planes)
        total = convolve(ah, w2, planes, 1)
        inputs = ax[(first + AHEAD) * FACE : (first + AHEAD + count) * FACE, centre].astype(F32)
        sums[first * FACE : (first + count) * FACE] = keep(total + inputs, planes)

    def place(n, carry):
        low = sums[pl.ds(pl.multiple_of(n * STEP, STEP), STEP)]
        high = sums[pl.ds(pl.multiple_of(ROWS // 2 + n * STEP, STEP), STEP)]
        for slot in range(2):
            chosen = jnp.where(down == slot, low, jnp.where(up == slot, high, 0.0))
            chosen = chosen.reshape(CHUNK, EDGE, EDGE, LANES)[..., :CH]
            out[slot, pl.ds(n * CHUNK, CHUNK)] = chosen.astype(BF16)
        return carry

    lax.fori_loop(0, 2, place, 0, unroll=True)

    for stage in (plane_add, line_add, plane_gather, core_gather):
        for g in range(2):
            stage(g)
    for copy in sent:
        copy.wait_send()


def unpack(packed, field, first, second, out):
    out[...] = field[...]
    for g, result in enumerate((first, second)):
        for tile in range(TILES_WIDE):
            turned = packed[g, CH * tile : CH * (tile + 1)].astype(F32).T
            count = min(LANES, WIDE - LANES * tile)
            result[LANES * tile : LANES * tile + count] = turned[:count]


def on_device(voxels, cotangent, weight_first, weight_second, act_count, up_list, down_list, table):
    vmem = pl.BlockSpec(memory_space=pltpu.VMEM)
    smem = pl.BlockSpec(memory_space=pltpu.SMEM)
    scale = 1.0 / math.sqrt(512 * 2 * EDGE**3)
    dma = pltpu.SemaphoreType.DMA
    field_shape = jax.ShapeDtypeStruct((2, EDGE, EDGE, EDGE, CH), BF16)
    packed_shape = jax.ShapeDtypeStruct((2, 2 * HALF, LANES), BF16)
    wide = pltpu.VMEM((ROWS + 2 * FACE, TILES_WIDE * LANES), BF16)
    wider = pltpu.VMEM((ROWS + 2 * AHEAD * FACE, TILES_WIDE * LANES), BF16)
    weight = pltpu.VMEM((27, CH, CH), BF16)
    bricks = pltpu.VMEM(field_shape.shape, BF16)
    turned = pltpu.VMEM((CH, ROWS), BF16)
    field, packed = pl.pallas_call(
        functools.partial(section, scale),
        out_shape=(field_shape, packed_shape),
        in_specs=[smem, smem] + [pl.BlockSpec(memory_space=pltpu.HBM)] * 4,
        out_specs=(vmem, vmem),
        scratch_shapes=[
            bricks, bricks, weight, weight, wider, wide, wide, weight,
            *[pltpu.VMEM((ROWS, LANES), F32)] * 3,
            turned, turned,
            *[pltpu.VMEM(((AHEAD + 1) * FACE + FLAG_ROWS, LANES), BF16)] * 4,
            pltpu.VMEM((2, 2 * HALF, LANES), F32),
            pltpu.VMEM((2, HALF, LANES), F32),
            pltpu.VMEM((2, SIZE_X * SIDE, SHARD, LANES), BF16),
            pltpu.VMEM((2, SIZE_X * SIDE, SHARD, LANES), BF16),
            pltpu.VMEM((2, SHARD, LANES), F32),
            pltpu.VMEM((2, SIDE, SHARD, LANES), F32),
            dma((4,)), dma((2,)), dma((2,)),
            *[dma((2, SIZE_X))] * 2, *[dma((2, SIZE_X * SIDE))] * 2,
            *[dma((2, SIDE))] * 2, *[dma((2, SIZE_X * SIDE))] * 2, *[dma((2, SIZE_X))] * 2,
        ],
        compiler_params=pltpu.CompilerParams(
            collective_id=0, has_side_effects=True, vmem_limit_bytes=48 * 2**20
        ),
        name="section",
    )(
        down_list, up_list,
        *[
            pltpu.with_memory_space_constraint(array, pltpu.HBM)
            for array in (voxels[0], cotangent[0], weight_first, weight_second)
        ],
    )
    step_rows = TILES_WIDE * CH
    first, second, out_field = pl.pallas_call(
        unpack,
        grid=(3,),
        out_shape=(jax.ShapeDtypeStruct((27 * CH, CH), F32),) * 2 + (field_shape,),
        in_specs=[
            pl.BlockSpec((2, step_rows, LANES), lambda i: (0, i, 0)),
            pl.BlockSpec(field_shape.shape, lambda i: (0, 0, 0, 0, 0)),
        ],
        out_specs=(
            pl.BlockSpec((WIDE, CH), lambda i: (i, 0)),
            pl.BlockSpec((WIDE, CH), lambda i: (i, 0)),
            pl.BlockSpec(field_shape.shape, lambda i: (0, 0, 0, 0, 0)),
        ),
        compiler_params=pltpu.CompilerParams(vmem_limit_bytes=32 * 2**20),
        name="unpack",
    )(packed, field)
    shape = weight_first.shape
    return (out_field[None], first.reshape(shape), second.reshape(shape))


def solution(mesh):
    in_specs = (
        P("rep", "space", None, None, None, None),
        P("rep", "space", None, None, None, None),
        P(),
        P(),
        P("rep", "space"),
        P("rep", "space"),
        P("rep", "space"),
        P("rep", "space", None),
    )
    out_specs = (P("rep", "space", None, None, None, None), P(), P())
    return jax.shard_map(
        on_device, mesh=mesh, in_specs=in_specs, out_specs=out_specs, check_vma=False
    )
```

```python
import functools
import math

import jax
import jax.numpy as jnp
from jax import lax
from jax.experimental import pallas as pl
from jax.experimental.pallas import tpu as pltpu
from jax.sharding import PartitionSpec as P

F32 = jnp.float32
BF16 = jnp.bfloat16
MESH = pl.DeviceIdType.MESH

SIZE_X, SIZE_Y, SIZE_Z = 4, 8, 8
EDGE = 8
CH = 96
LANES = 128
FACE = EDGE * EDGE
PLANES = 2 * EDGE
ROWS = PLANES * FACE
WIDE = 9 * CH
TILES_WIDE = 7
HALF = 1024
GROUP = HALF // SIZE_X
SIDE = 8
SHARD = GROUP // SIDE
STEPS_X = (2, 1, 3, 0)
STEPS = (4, 3, 5, 2, 6, 1, 7)
PLANE = tuple((a, b) for a in STEPS_X for b in STEPS + (0,) if a or b)
FLAG_ROWS = 16
AHEAD = 2
CHUNK = 4
STEP = CHUNK * FACE


def widen(value):
    value = value.astype(F32)
    blank = jnp.zeros(value.shape[:-1] + (LANES - CH,), F32)
    return jnp.concatenate([value, blank], axis=-1)


def spread(value, out, row):
    planes = value.shape[0]
    flat = value.reshape(planes * EDGE, EDGE, LANES)
    depth = lax.broadcasted_iota(jnp.int32, flat.shape, 1)
    by_depth = [
        jnp.where(depth == 0, 0.0, pltpu.roll(flat, 1, 1)),
        flat,
        jnp.where(depth == EDGE - 1, 0.0, pltpu.roll(flat, EDGE - 1, 1)),
    ]

    def piece(index):
        shift_y, shift_z = index // 3, index % 3
        turned = by_depth[shift_z]
        turn = CH * index % LANES
        if turn:
            turned = pltpu.roll(turned, turn, 2)
        turned = turned.reshape(planes, EDGE, EDGE, LANES)
        blank = jnp.zeros((planes, 1, EDGE, LANES), F32)
        if shift_y == 0:
            turned = jnp.concatenate([blank, turned[:, : EDGE - 1]], axis=1)
        elif shift_y == 2:
            turned = jnp.concatenate([turned[:, 1:], blank], axis=1)
        return turned.reshape(planes * FACE, LANES)

    lane = lax.broadcasted_iota(jnp.int32, (planes * FACE, LANES), 1)
    pieces = [piece(index) for index in range(9)]
    for tile in range(TILES_WIDE):
        first = LANES * tile // CH
        border = CH * (first + 1) - LANES * tile
        block = pieces[first]
        if border < LANES and first + 1 < 9:
            block = jnp.where(lane < border, block, pieces[first + 1])
        out[pl.ds(row, planes * FACE), LANES * tile : LANES * (tile + 1)] = block.astype(BF16)


def section(
    scale,
    down_ref, up_ref, vox_hbm, cot_hbm, w1_hbm, w2_hbm,
    out, grad_first, grad_second,
    vox, cot, w1, w2, ax, ah, ag, wt, dslope, slopes, sums, st, ct,
    up_send, down_send, from_lo, from_hi,
    part_sum, core_in, plane_out, plane_in, mid, cross, packed,
    load_s, halo_s, halo_r, s0, r0, s1, r1, s2, r2, s3, r3, s4, r4,
):
    space = lax.axis_index("space")
    rep = lax.axis_index("rep")
    owners = SIZE_X * SIZE_Z * 2
    y_lo = lax.rem(space, 2)
    my_z = lax.rem(lax.div(space, 2), SIZE_Z)
    my_x = lax.div(space, 2 * SIZE_Z)
    core = lax.rem(rep, 2)
    my_y = lax.div(rep, 2) * 2 + y_lo

    def device(x, y, z, c):
        return ((x * SIZE_Z + z) * 2 + lax.rem(y, 2), lax.div(y, 2) * 2 + c)

    side = my_z * (1 - core) + my_y * core
    line = my_y * (1 - core) + my_z * core

    def in_plane(x, t):
        return device(x, my_y * (1 - core) + t * core, t * (1 - core) + my_z * core, core)

    def in_line(t):
        return device(my_x, t * (1 - core) + my_y * core, my_z * (1 - core) + t * core, core)

    def moved(a, b):
        return lax.rem(my_x + a, SIZE_X), lax.rem(side + b, SIDE)

    twin = device(my_x, my_y, my_z, 1 - core)
    above = (lax.rem(space + 1, owners), rep)
    below = (lax.rem(space + owners - 1, owners), rep)

    def send(src, dst, send_sem, recv_sem, target):
        copy = pltpu.make_async_remote_copy(
            src_ref=src, dst_ref=dst, send_sem=send_sem, recv_sem=recv_sem,
            device_id=target, device_id_type=MESH,
        )
        copy.start()
        return copy

    def arrived(dst, send_sem, recv_sem, target):
        pltpu.make_async_remote_copy(
            src_ref=dst, dst_ref=dst, send_sem=send_sem, recv_sem=recv_sem,
            device_id=target, device_id_type=MESH,
        ).wait_recv()

    loads = [
        pltpu.make_async_copy(src, dst, load_s.at[n])
        for n, (src, dst) in enumerate(
            ((vox_hbm, vox), (cot_hbm, cot), (w1_hbm, w1), (w2_hbm, w2))
        )
    ]
    for load in loads:
        load.start()

    barrier = pltpu.get_barrier_semaphore()
    partners = [above, below, twin]
    partners += [in_plane(*moved(a, b)) for a, b in PLANE]
    partners += [in_line(lax.rem(line + d, SIDE)) for d in STEPS]
    for partner in partners:
        pl.semaphore_signal(barrier, inc=1, device_id=partner, device_id_type=MESH)

    down = down_ref[0, 0]
    up = up_ref[0, 0]
    sent = []

    def face(field, slot, plane):
        first, second = widen(field[0, plane]), widen(field[1, plane])
        chosen = jnp.where(slot == 0, first, jnp.where(slot == 1, second, 0.0))
        return chosen.reshape(FACE, LANES).astype(BF16)

    loads[0].wait()
    loads[1].wait()
    faces = ((vox, EDGE - 2, 0), (vox, EDGE - 1, 1), (cot, EDGE - 1, 0))
    for at, (field, high, low) in enumerate(faces):
        up_send[at * FACE : (at + 1) * FACE] = face(field, up, high)
        down_send[at * FACE : (at + 1) * FACE] = face(field, down, low)
    flags = (AHEAD + 1) * FACE
    for buffer, slot in ((up_send, up), (down_send, down)):
        buffer[flags:] = jnp.where(slot < 2, 1.0, 0.0) * jnp.ones((FLAG_ROWS, LANES), BF16)
    pl.semaphore_wait(barrier, len(partners))
    sent.append(send(up_send, from_lo, halo_s.at[0], halo_r.at[0], above))
    sent.append(send(down_send, from_hi, halo_s.at[1], halo_r.at[1], below))

    def fill(field, wide, ahead):
        def body(c, carry):
            planes = pl.ds(lax.rem(c, 2) * CHUNK, CHUNK)
            slot = jnp.where(c < 2, down, up)
            first, second = widen(field[0, planes]), widen(field[1, planes])
            chosen = jnp.where(slot == 0, first, jnp.where(slot == 1, second, 0.0))
            spread(chosen, wide, pl.multiple_of(ahead * FACE + c * STEP, FACE))
            return carry

        lax.fori_loop(0, 4, body, 0, unroll=True)

    def weights(n, carry):
        for k in range(3):
            o = 3 * n + k
            own = widen(w2[o])
            square = jnp.concatenate([own, jnp.zeros((LANES - CH, LANES), F32)], axis=0)
            wt[26 - o] = square.T[:CH, :CH].astype(BF16)
        return carry

    lower_valid = space > 0
    upper_valid = space < owners - 1

    def cot_turn(c, carry):
        block = ag[pl.ds(pl.multiple_of(FACE + c * STEP, FACE), STEP), 3 * LANES : 4 * LANES]
        ct[:, pl.ds(pl.multiple_of(c * STEP, STEP), STEP)] = block.astype(F32).T[:CH].astype(BF16)
        return carry

    def neighbour(buffer, valid):
        flag = buffer[flags : flags + FLAG_ROWS].astype(F32)[:1]
        return jnp.where(valid, flag, 0.0) > 0.5

    def keep(value, planes):
        kept = []
        for k, plane in enumerate(planes):
            if plane < 0:
                active = neighbour(from_lo, lower_valid)
            elif plane >= PLANES:
                active = neighbour(from_hi, upper_valid)
            else:
                active = (down if plane < EDGE else up) < 2
            kept.append(jnp.where(active, value[k * FACE : (k + 1) * FACE], 0.0))
        return jnp.concatenate(kept, axis=0)

    def runs(planes):
        found = []
        for k, plane in enumerate(planes):
            if k and plane == planes[k - 1] + 1:
                found[-1][2] += 1
            else:
                found.append([k, plane, 1])
        return found

    def convolve(wide, weight, planes, ahead):
        total = None
        for i in range(3):
            rows = [
                wide[(first + ahead - 1 + i) * FACE : (first + ahead - 1 + i + count) * FACE, :WIDE]
                for _, first, count in runs(planes)
            ]
            product = jnp.dot(
                rows[0] if len(rows) == 1 else jnp.concatenate(rows, axis=0),
                weight[9 * i : 9 * i + 9].reshape(WIDE, CH),
                preferred_element_type=F32,
            )
            total = product if total is None else total + product
        return widen(total)

    def first_conv(planes):
        before = keep(convolve(ax, w1, planes, AHEAD), planes)
        gate = jax.nn.sigmoid(before)
        factor = gate * (1.0 + before * (1.0 - gate))
        hidden = (before * gate).astype(BF16).astype(F32)
        for k, plane in enumerate(planes):
            if 0 <= plane < PLANES:
                dslope[plane * FACE : (plane + 1) * FACE] = factor[k * FACE : (k + 1) * FACE]
        for k, first, count in runs(planes):
            block = hidden[k * FACE : (k + count) * FACE].reshape(count, EDGE, EDGE, LANES)
            spread(block, ah, (first + 1) * FACE)

    def through(planes):
        total = keep(convolve(ag, wt, planes, 1), planes)
        for k, first, count in runs(planes):
            rows = slice(first * FACE, (first + count) * FACE)
            slopes[rows] = total[k * FACE : (k + count) * FACE] * dslope[rows]

    def turn(pairs):
        for pair in pairs:
            rows = slice(pair * 2 * FACE, (pair + 1) * 2 * FACE)
            st[:, rows] = slopes[rows].T[:CH].astype(BF16)

    def gradient(turned, wide, g, ahead, k, inside):
        i = k * core + (2 - k) * (1 - core)

        def rows(plane, count):
            return pl.ds(pl.multiple_of((i + ahead - 1 + plane) * FACE, FACE), count * FACE)

        if inside:
            left, right = turned[:, 2 * FACE : 14 * FACE], wide[rows(2, 12)]
        else:
            left = jnp.concatenate([turned[:, : 2 * FACE], turned[:, 14 * FACE :]], axis=1)
            right = jnp.concatenate([wide[rows(0, 2)], wide[rows(14, 2)]], axis=0)
        block = jnp.dot(left, right, preferred_element_type=F32)
        for tile in range(TILES_WIDE):
            at = pl.ds(pl.multiple_of((i * TILES_WIDE + tile) * CH, CH), CH)
            part = block[:, LANES * tile : LANES * (tile + 1)]
            part_sum[g, at] = part if inside else part_sum[g, at] + part

    fill(vox, ax, AHEAD)
    inner = ((1, 2, 3, 4), (5, 6, 7), (8, 9, 10), (11, 12, 13, 14))
    loads[2].wait()
    for planes in inner:
        first_conv(planes)
    loads[3].wait()
    lax.fori_loop(0, 9, weights, 0, unroll=True)
    fill(cot, ag, 1)
    lax.fori_loop(0, 4, cot_turn, 0, unroll=True)
    for planes in inner:
        through(planes)
    turn(range(1, 7))
    used = 3 * TILES_WIDE * CH
    for g in range(2):
        part_sum[g, used:] = jnp.zeros((2 * HALF - used, LANES), F32)
    for k in range(3):
        gradient(st, ax, 0, AHEAD, k, True)
    for k in range(3):
        gradient(ct, ah, 1, 1, k, True)

    def edge_in(buffer, at, count, valid, wide, row):
        block = buffer[at * FACE : (at + count) * FACE].astype(F32)
        block = jnp.where(valid, block, 0.0).reshape(count, EDGE, EDGE, LANES)
        spread(block, wide, row)

    arrived(from_lo, halo_s.at[0], halo_r.at[0], above)
    arrived(from_hi, halo_s.at[1], halo_r.at[1], below)
    edge_in(from_lo, 0, AHEAD, lower_valid, ax, 0)
    edge_in(from_hi, 0, AHEAD, upper_valid, ax, (PLANES + AHEAD) * FACE)
    first_conv((-1, 0, 15, 16))
    edge_in(from_lo, AHEAD, 1, lower_valid, ag, 0)
    edge_in(from_hi, AHEAD, 1, upper_valid, ag, (PLANES + 1) * FACE)
    through((0, 15))
    turn((0, 7))
    centre = slice(3 * LANES, 4 * LANES)

    def rows_of(start, count):
        return pl.ds(pl.multiple_of(start, SHARD), count)

    def other(k, me):
        return k + jnp.where(k >= me, 1, 0)

    def core_send(g):
        src = part_sum.at[g, rows_of((1 - core) * HALF, HALF)]
        sent.append(send(src, core_in.at[g], s0.at[g], r0.at[g], twin))

    def all_sent(src, sem):
        pltpu.make_async_copy(src, src, sem).wait()

    def core_add(g):
        arrived(core_in.at[g], s0.at[g], r0.at[g], twin)
        for n, (a, b) in enumerate(PLANE):
            x, t = moved(a, b)
            at = x * GROUP + t * SHARD
            total = part_sum[g, rows_of(core * HALF + at, SHARD)] + core_in[g, rows_of(at, SHARD)]
            plane_out[g, n] = total.astype(BF16)
            send(plane_out.at[g, n], plane_in.at[g, n], s1.at[g], r1.at[g], in_plane(x, t))
        at = my_x * GROUP + side * SHARD
        mid[g] = part_sum[g, rows_of(core * HALF + at, SHARD)] + core_in[g, rows_of(at, SHARD)]

    def plane_add(g):
        arrived(plane_in.at[g], s1.at[g], r1.at[g], twin)
        total = mid[g]
        for n in range(len(PLANE)):
            total = total + plane_in[g, n].astype(F32)
        cross[g, line] = total
        mine = cross.at[g, line]
        for k in range(SIDE - 1):
            send(mine, mine, s2.at[g], r2.at[g], in_line(other(k, line)))

    def line_add(g):
        arrived(cross.at[g, : SIDE - 1], s2.at[g], r2.at[g], twin)
        total = cross[g, 0]
        for t in range(1, SIDE):
            total = total + cross[g, t]
        rows = rows_of(core * HALF + my_x * GROUP + side * SHARD, SHARD)
        packed[g, rows] = (total * scale).astype(BF16)
        mine = packed.at[g, rows]
        me = side * SIZE_X + my_x
        for k in range(SIDE * SIZE_X - 1):
            at = other(k, me)
            target = in_plane(lax.rem(at, SIZE_X), lax.div(at, SIZE_X))
            send(mine, mine, s3.at[g], r3.at[g, my_x], target)

    def plane_gather(g):
        for a in STEPS_X[::-1]:
            x = lax.rem(my_x + SIZE_X - a, SIZE_X)
            count = GROUP if a else GROUP - SHARD
            arrived(packed.at[g, rows_of(core * HALF + x * GROUP, count)], s3.at[g], r3.at[g, x], twin)
            group = packed.at[g, rows_of(core * HALF + x * GROUP, GROUP)]
            sent.append(send(group, group, s4.at[g, a], r4.at[g, a], twin))

    def core_gather(g):
        for a in STEPS_X[::-1]:
            x = lax.rem(my_x + SIZE_X - a, SIZE_X)
            group = packed.at[g, rows_of((1 - core) * HALF + x * GROUP, GROUP)]
            arrived(group, s4.at[g, a], r4.at[g, a], twin)
        result = (grad_first, grad_second)[g]
        for i in range(3):
            for tile in range(TILES_WIDE):
                at = (i * TILES_WIDE + tile) * CH
                count = min(LANES, WIDE - LANES * tile)
                start = i * WIDE + LANES * tile
                result[start : start + count] = packed[g, at : at + CH].astype(F32).T[:count]

    gradient(st, ax, 0, AHEAD, 0, False)
    gradient(st, ax, 0, AHEAD, 1, False)
    core_send(0)
    gradient(st, ax, 0, AHEAD, 2, False)
    gradient(ct, ah, 1, 1, 0, False)
    gradient(ct, ah, 1, 1, 1, False)
    core_send(1)
    core_add(0)
    gradient(ct, ah, 1, 1, 2, False)
    core_add(1)

    for planes in ((0, 1, 2, 3), (4, 5, 6, 7), (8, 9, 10, 11), (12, 13, 14, 15)):
        first, count = planes[0], len(planes)
        total = convolve(ah, w2, planes, 1)
        inputs = ax[(first + AHEAD) * FACE : (first + AHEAD + count) * FACE, centre].astype(F32)
        sums[first * FACE : (first + count) * FACE] = keep(total + inputs, planes)

    def place(n, carry):
        low = sums[pl.ds(pl.multiple_of(n * STEP, STEP), STEP)]
        high = sums[pl.ds(pl.multiple_of(ROWS // 2 + n * STEP, STEP), STEP)]
        for slot in range(2):
            chosen = jnp.where(down == slot, low, jnp.where(up == slot, high, 0.0))
            chosen = chosen.reshape(CHUNK, EDGE, EDGE, LANES)[..., :CH]
            out[slot, pl.ds(n * CHUNK, CHUNK)] = chosen.astype(BF16)
        return carry

    lax.fori_loop(0, 2, place, 0, unroll=True)

    for stage in (plane_add, line_add, plane_gather, core_gather):
        for g in range(2):
            stage(g)
    for copy in sent:
        copy.wait_send()
    for g in range(2):
        all_sent(plane_out.at[g], s1.at[g])
        all_sent(cross.at[g, : SIDE - 1], s2.at[g])
        all_sent(packed.at[g, : HALF - SHARD], s3.at[g])


def store(*refs):
    count = len(refs) // 2
    copies = [
        pltpu.make_async_copy(src, dst, refs[-1].at[n])
        for n, (src, dst) in enumerate(zip(refs[:count], refs[count : 2 * count]))
    ]
    for copy in copies:
        copy.start()
    for copy in copies:
        copy.wait()


def on_device(voxels, cotangent, weight_first, weight_second, act_count, up_list, down_list, table):
    vmem = pl.BlockSpec(memory_space=pltpu.VMEM)
    smem = pl.BlockSpec(memory_space=pltpu.SMEM)
    scale = 1.0 / math.sqrt(512 * 2 * EDGE**3)
    dma = pltpu.SemaphoreType.DMA
    field_shape = jax.ShapeDtypeStruct((2, EDGE, EDGE, EDGE, CH), BF16)
    sum_shape = jax.ShapeDtypeStruct((27 * CH, CH), F32)
    results = (field_shape, sum_shape, sum_shape)
    wide = pltpu.VMEM((ROWS + 2 * FACE, TILES_WIDE * LANES), BF16)
    wider = pltpu.VMEM((ROWS + 2 * AHEAD * FACE, TILES_WIDE * LANES), BF16)
    weight = pltpu.VMEM((27, CH, CH), BF16)
    bricks = pltpu.VMEM(field_shape.shape, BF16)
    turned = pltpu.VMEM((CH, ROWS), BF16)
    held = pl.pallas_call(
        functools.partial(section, scale),
        out_shape=results,
        in_specs=[smem, smem] + [pl.BlockSpec(memory_space=pltpu.HBM)] * 4,
        out_specs=(vmem,) * 3,
        scratch_shapes=[
            bricks, bricks, weight, weight, wider, wide, wide, weight,
            *[pltpu.VMEM((ROWS, LANES), F32)] * 3,
            turned, turned,
            *[pltpu.VMEM(((AHEAD + 1) * FACE + FLAG_ROWS, LANES), BF16)] * 4,
            pltpu.VMEM((2, 2 * HALF, LANES), F32),
            pltpu.VMEM((2, HALF, LANES), F32),
            *[pltpu.VMEM((2, len(PLANE), SHARD, LANES), BF16)] * 2,
            pltpu.VMEM((2, SHARD, LANES), F32),
            pltpu.VMEM((2, SIDE, SHARD, LANES), F32),
            pltpu.VMEM((2, 2 * HALF, LANES), BF16),
            dma((4,)), dma((2,)), dma((2,)),
            *[dma((2,))] * 7, dma((2, SIZE_X)), *[dma((2, SIZE_X))] * 2,
        ],
        compiler_params=pltpu.CompilerParams(
            collective_id=0, has_side_effects=True, vmem_limit_bytes=48 * 2**20
        ),
        name="section",
    )(
        down_list, up_list,
        *[
            pltpu.with_memory_space_constraint(array, pltpu.HBM)
            for array in (voxels[0], cotangent[0], weight_first, weight_second)
        ],
    )
    out_field, first, second = pl.pallas_call(
        store,
        out_shape=results,
        in_specs=[vmem] * 3,
        out_specs=(pl.BlockSpec(memory_space=pltpu.HBM),) * 3,
        scratch_shapes=[dma((3,))],
        compiler_params=pltpu.CompilerParams(vmem_limit_bytes=8 * 2**20),
        name="store",
    )(*held)
    shape = weight_first.shape
    return (out_field[None], first.reshape(shape), second.reshape(shape))


def solution(mesh):
    in_specs = (
        P("rep", "space", None, None, None, None),
        P("rep", "space", None, None, None, None),
        P(),
        P(),
        P("rep", "space"),
        P("rep", "space"),
        P("rep", "space"),
        P("rep", "space", None),
    )
    out_specs = (P("rep", "space", None, None, None, None), P(), P())
    return jax.shard_map(
        on_device, mesh=mesh, in_specs=in_specs, out_specs=out_specs, check_vma=False
    )
```

```python
import functools
import math

import jax
import jax.numpy as jnp
from jax import lax
from jax.experimental import pallas as pl
from jax.experimental.pallas import tpu as pltpu
from jax.sharding import PartitionSpec as P

F32 = jnp.float32
BF16 = jnp.bfloat16
MESH = pl.DeviceIdType.MESH

SIZE_X, SIZE_Y, SIZE_Z = 4, 8, 8
EDGE = 8
CH = 96
LANES = 128
FACE = EDGE * EDGE
PLANES = 2 * EDGE
ROWS = PLANES * FACE
WIDE = 9 * CH
TALL = 3 * CH
TILES_WIDE = 7
HALF = 1024
GROUP = HALF // SIZE_X
SIDE = 8
SHARD = GROUP // SIDE
STEPS_X = (2, 1, 3, 0)
STEPS = (4, 3, 5, 2, 6, 1, 7)
PLANE = tuple((a, b) for a in STEPS_X for b in STEPS + (0,) if a or b)
FLAG_ROWS = 16
AHEAD = 2
CHUNK = 4
STEP = CHUNK * FACE


def widen(value):
    value = value.astype(F32)
    blank = jnp.zeros(value.shape[:-1] + (LANES - CH,), F32)
    return jnp.concatenate([value, blank], axis=-1)


def shifted(value, step):
    if step == 0:
        return value
    deep = value.reshape(-1, EDGE, LANES)
    depth = lax.broadcasted_iota(jnp.int32, deep.shape, 1)
    if step > 0:
        moved = jnp.where(depth == EDGE - 1, 0.0, pltpu.roll(deep, EDGE - 1, 1))
    else:
        moved = jnp.where(depth == 0, 0.0, pltpu.roll(deep, 1, 1))
    return moved.reshape(value.shape)


def spread(value, out, row):
    planes = value.shape[0] - 2
    flat = value.reshape(-1, LANES)
    turns = {turn: pltpu.roll(flat, turn, 1).reshape(value.shape) for turn in (32, 64, 96)}
    turns[0] = value

    def piece(index):
        shift_x, shift_y = index // 3, index % 3
        turned = turns[CH * index % LANES][shift_x : shift_x + planes]
        blank = jnp.zeros((planes, 1, EDGE, LANES), F32)
        if shift_y == 0:
            turned = jnp.concatenate([blank, turned[:, : EDGE - 1]], axis=1)
        elif shift_y == 2:
            turned = jnp.concatenate([turned[:, 1:], blank], axis=1)
        return turned.reshape(planes * FACE, LANES)

    lane = lax.broadcasted_iota(jnp.int32, (planes * FACE, LANES), 1)
    pieces = [piece(index) for index in range(9)]
    for tile in range(TILES_WIDE):
        first = LANES * tile // CH
        border = CH * (first + 1) - LANES * tile
        block = pieces[first]
        if border < LANES and first + 1 < 9:
            block = jnp.where(lane < border, block, pieces[first + 1])
        out[row : row + planes * FACE, LANES * tile : LANES * (tile + 1)] = block.astype(BF16)


def section(
    scale,
    down_ref, up_ref, vox_hbm, cot_hbm, w1_hbm, w2_hbm,
    out, grad_first, grad_second,
    vox, cot, w1, w2, fx, fh, fg, bx, bh, bg, c1, c2, ct2, dslope, slopes, sums, st, ct,
    up_send, down_send, from_lo, from_hi,
    part_sum, core_in, plane_out, plane_in, mid, cross, packed,
    load_s, halo_s, halo_r, s0, r0, s1, r1, s2, r2, s3, r3, s4, r4,
):
    space = lax.axis_index("space")
    rep = lax.axis_index("rep")
    owners = SIZE_X * SIZE_Z * 2
    y_lo = lax.rem(space, 2)
    my_z = lax.rem(lax.div(space, 2), SIZE_Z)
    my_x = lax.div(space, 2 * SIZE_Z)
    core = lax.rem(rep, 2)
    my_y = lax.div(rep, 2) * 2 + y_lo

    def device(x, y, z, c):
        return ((x * SIZE_Z + z) * 2 + lax.rem(y, 2), lax.div(y, 2) * 2 + c)

    side = my_z * (1 - core) + my_y * core
    line = my_y * (1 - core) + my_z * core

    def in_plane(x, t):
        return device(x, my_y * (1 - core) + t * core, t * (1 - core) + my_z * core, core)

    def in_line(t):
        return device(my_x, t * (1 - core) + my_y * core, my_z * (1 - core) + t * core, core)

    def moved(a, b):
        return lax.rem(my_x + a, SIZE_X), lax.rem(side + b, SIDE)

    twin = device(my_x, my_y, my_z, 1 - core)
    above = (lax.rem(space + 1, owners), rep)
    below = (lax.rem(space + owners - 1, owners), rep)

    def send(src, dst, send_sem, recv_sem, target):
        copy = pltpu.make_async_remote_copy(
            src_ref=src, dst_ref=dst, send_sem=send_sem, recv_sem=recv_sem,
            device_id=target, device_id_type=MESH,
        )
        copy.start()
        return copy

    def arrived(dst, send_sem, recv_sem, target):
        pltpu.make_async_remote_copy(
            src_ref=dst, dst_ref=dst, send_sem=send_sem, recv_sem=recv_sem,
            device_id=target, device_id_type=MESH,
        ).wait_recv()

    loads = [
        pltpu.make_async_copy(src, dst, load_s.at[n])
        for n, (src, dst) in enumerate(
            ((vox_hbm, vox), (cot_hbm, cot), (w1_hbm, w1), (w2_hbm, w2))
        )
    ]
    for load in loads[:2]:
        load.start()

    barrier = pltpu.get_barrier_semaphore()
    partners = [above, below, twin]
    partners += [in_plane(*moved(a, b)) for a, b in PLANE]
    partners += [in_line(lax.rem(line + d, SIDE)) for d in STEPS]
    for partner in partners:
        pl.semaphore_signal(barrier, inc=1, device_id=partner, device_id_type=MESH)

    for load in loads[2:]:
        load.start()
    down = down_ref[0, 0]
    up = up_ref[0, 0]
    sent = []
    for joined in (c1, c2, ct2):
        joined[...] = jnp.zeros(joined.shape, BF16)

    def fill(field, planes, ahead):
        for slot, start in ((down, 0), (up, EDGE)):
            for at in range(0, EDGE, CHUNK):
                one, two = (widen(field[n, at : at + CHUNK]) for n in range(2))
                chosen = jnp.where(slot == 0, one, jnp.where(slot == 1, two, 0.0))
                row = (ahead + start + at) * FACE
                planes[row : row + STEP] = chosen.reshape(STEP, LANES)

    loads[0].wait()
    fill(vox, fx, AHEAD)
    loads[1].wait()
    fill(cot, fg, 1)
    flags = (AHEAD + 1) * FACE
    for buffer, slot, high, low in (
        (up_send, up, PLANES - AHEAD, PLANES - 1), (down_send, down, 0, 0)
    ):
        row = (AHEAD + high) * FACE
        buffer[: AHEAD * FACE] = fx[row : row + AHEAD * FACE].astype(BF16)
        buffer[AHEAD * FACE : flags] = fg[(1 + low) * FACE : (2 + low) * FACE].astype(BF16)
        buffer[flags:] = jnp.where(slot < 2, 1.0, 0.0) * jnp.ones((FLAG_ROWS, LANES), BF16)
    pl.semaphore_wait(barrier, len(partners))
    sent.append(send(up_send, from_lo, halo_s.at[0], halo_r.at[0], above))
    sent.append(send(down_send, from_hi, halo_s.at[1], halo_r.at[1], below))

    def join(offset, value, joined):
        pair, depth = offset // 3, offset % 3
        joined[pair * CH : (pair + 1) * CH, LANES * depth : LANES * depth + CH] = value

    lower_valid = space > 0
    upper_valid = space < owners - 1

    def neighbour(buffer, valid):
        flag = buffer[flags : flags + FLAG_ROWS].astype(F32)[:1]
        return jnp.where(valid, flag, 0.0) > 0.5

    def keep(value, planes):
        kept = []
        for k, plane in enumerate(planes):
            if plane < 0:
                active = neighbour(from_lo, lower_valid)
            elif plane >= PLANES:
                active = neighbour(from_hi, upper_valid)
            else:
                active = (down if plane < EDGE else up) < 2
            kept.append(jnp.where(active, value[k * FACE : (k + 1) * FACE], 0.0))
        return jnp.concatenate(kept, axis=0)

    def runs(planes):
        found = []
        for k, plane in enumerate(planes):
            if k and plane == planes[k - 1] + 1:
                found[-1][2] += 1
            else:
                found.append([k, plane, 1])
        return found

    def widened(source, ahead, wide, wide_ahead, planes):
        for _, first, count in runs(planes):
            rows = slice((first - 1 + ahead) * FACE, (first + 1 + count + ahead) * FACE)
            value = source[rows].reshape(count + 2, EDGE, EDGE, LANES)
            spread(value, wide, (first + wide_ahead) * FACE)

    def convolve(wide, joined, planes, ahead):
        rows = [
            wide[(first + ahead) * FACE : (first + ahead + count) * FACE, :WIDE]
            for _, first, count in runs(planes)
        ]
        rows = rows[0] if len(rows) == 1 else jnp.concatenate(rows, axis=0)
        product = jnp.dot(rows, joined[...], preferred_element_type=F32)
        parts = [product[:, LANES * k : LANES * (k + 1)] for k in range(3)]
        return shifted(parts[0], -1) + parts[1] + shifted(parts[2], 1)

    def first_conv(planes):
        widened(fx, AHEAD, bx, 1, planes)
        before = keep(convolve(bx, c1, planes, 1), planes)
        gate = jax.nn.sigmoid(before)
        factor = gate * (1.0 + before * (1.0 - gate))
        hidden = (before * gate).astype(BF16).astype(F32)
        for k, plane in enumerate(planes):
            part = slice(k * FACE, (k + 1) * FACE)
            if 0 <= plane < PLANES:
                dslope[plane * FACE : (plane + 1) * FACE] = factor[part]
            fh[(plane + 1) * FACE : (plane + 2) * FACE] = hidden[part]

    def through(planes):
        widened(fg, 1, bg, 0, planes)
        total = keep(convolve(bg, ct2, planes, 0), planes)
        for k, first, count in runs(planes):
            rows = slice(first * FACE, (first + count) * FACE)
            slopes[rows] = total[k * FACE : (k + count) * FACE] * dslope[rows]

    def turn(source, ahead, turned, pairs):
        for pair in pairs:
            rows = slice(pair * 2 * FACE, (pair + 1) * 2 * FACE)
            value = source[(2 * pair + ahead) * FACE : (2 * pair + 2 + ahead) * FACE]
            for depth in range(3):
                block = shifted(value, 1 - depth).T[:CH]
                turned[depth * CH : (depth + 1) * CH, rows] = block.astype(BF16)

    def gradient(turned, wide, g, ahead, inside):
        def rows(plane, count):
            return slice((ahead + plane) * FACE, (ahead + plane + count) * FACE)

        if inside:
            left, right = turned[:, 2 * FACE : 14 * FACE], wide[rows(2, 12)]
        else:
            left = jnp.concatenate([turned[:, : 2 * FACE], turned[:, 14 * FACE :]], axis=1)
            right = jnp.concatenate([wide[rows(0, 2)], wide[rows(14, 2)]], axis=0)
        block = jnp.dot(left, right, preferred_element_type=F32)
        for tile in range(TILES_WIDE):
            at = slice(tile * TALL, (tile + 1) * TALL)
            part = block[:, LANES * tile : LANES * (tile + 1)]
            part_sum[g, at] = part if inside else part_sum[g, at] + part

    inner = ((1, 2, 3, 4), (5, 6, 7), (8, 9, 10), (11, 12, 13, 14))
    loads[2].wait()
    for offset in range(27):
        join(offset, w1[offset], c1)
    for planes in inner:
        first_conv(planes)
    loads[3].wait()
    for offset in range(27):
        own = widen(w2[offset])
        square = jnp.concatenate([own, jnp.zeros((LANES - CH, LANES), F32)], axis=0)
        join(26 - offset, square.T[:CH, :CH].astype(BF16), ct2)
    for planes in inner:
        through(planes)
    turn(fg, 1, ct, range(8))
    turn(slopes, 0, st, range(1, 7))
    for planes in ((2, 3, 4), (5, 6, 7), (8, 9, 10), (11, 12, 13)):
        widened(fh, 1, bh, 0, planes)
    used = TILES_WIDE * TALL
    for g in range(2):
        part_sum[g, used:] = jnp.zeros((2 * HALF - used, LANES), F32)
    gradient(st, bx, 0, 1, True)
    gradient(ct, bh, 1, 0, True)
    for offset in range(27):
        join(offset, w2[offset], c2)

    def edge_in(buffer, at, count, valid, planes, row):
        block = buffer[at * FACE : (at + count) * FACE].astype(F32)
        planes[row : row + count * FACE] = jnp.where(valid, block, 0.0)

    arrived(from_lo, halo_s.at[0], halo_r.at[0], above)
    arrived(from_hi, halo_s.at[1], halo_r.at[1], below)
    edge_in(from_lo, 0, AHEAD, lower_valid, fx, 0)
    edge_in(from_hi, 0, AHEAD, upper_valid, fx, (PLANES + AHEAD) * FACE)
    edge_in(from_lo, AHEAD, 1, lower_valid, fg, 0)
    edge_in(from_hi, AHEAD, 1, upper_valid, fg, (PLANES + 1) * FACE)
    first_conv((-1, 0, 15, 16))
    through((0, 15))
    turn(slopes, 0, st, (0, 7))
    widened(fh, 1, bh, 0, (0, 1, 14, 15))

    def rows_of(start, count):
        return pl.ds(pl.multiple_of(start, SHARD), count)

    def other(k, me):
        return k + jnp.where(k >= me, 1, 0)

    def core_send(g):
        for a in STEPS_X:
            start = lax.rem(my_x + a, SIZE_X) * GROUP
            src = part_sum.at[g, rows_of((1 - core) * HALF + start, GROUP)]
            dst = core_in.at[g, rows_of(start, GROUP)]
            sent.append(send(src, dst, s0.at[g, a], r0.at[g, a], twin))

    def all_sent(src, sem):
        pltpu.make_async_copy(src, src, sem).wait()

    def core_add(g):
        for n, (a, b) in enumerate(PLANE):
            x, t = moved(a, b)
            if b == STEPS[0]:
                group = core_in.at[g, rows_of(x * GROUP, GROUP)]
                arrived(group, s0.at[g, a], r0.at[g, a], twin)
            at = x * GROUP + t * SHARD
            total = part_sum[g, rows_of(core * HALF + at, SHARD)] + core_in[g, rows_of(at, SHARD)]
            plane_out[g, n] = total.astype(BF16)
            send(plane_out.at[g, n], plane_in.at[g, n], s1.at[g], r1.at[g], in_plane(x, t))
        at = my_x * GROUP + side * SHARD
        mid[g] = part_sum[g, rows_of(core * HALF + at, SHARD)] + core_in[g, rows_of(at, SHARD)]

    def plane_add(g):
        arrived(plane_in.at[g], s1.at[g], r1.at[g], twin)
        total = mid[g]
        for n in range(len(PLANE)):
            total = total + plane_in[g, n].astype(F32)
        cross[g, line] = total
        mine = cross.at[g, line]
        for k in range(SIDE - 1):
            send(mine, mine, s2.at[g], r2.at[g], in_line(other(k, line)))

    def line_add(g):
        arrived(cross.at[g, : SIDE - 1], s2.at[g], r2.at[g], twin)
        total = cross[g, 0]
        for t in range(1, SIDE):
            total = total + cross[g, t]
        rows = rows_of(core * HALF + my_x * GROUP + side * SHARD, SHARD)
        packed[g, rows] = (total * scale).astype(BF16)
        mine = packed.at[g, rows]
        me = side * SIZE_X + my_x
        for k in range(SIDE * SIZE_X - 1):
            at = other(k, me)
            target = in_plane(lax.rem(at, SIZE_X), lax.div(at, SIZE_X))
            send(mine, mine, s3.at[g], r3.at[g, my_x], target)

    def plane_gather(g):
        for a in STEPS_X[::-1]:
            x = lax.rem(my_x + SIZE_X - a, SIZE_X)
            count = GROUP if a else GROUP - SHARD
            arrived(packed.at[g, rows_of(core * HALF + x * GROUP, count)], s3.at[g], r3.at[g, x], twin)
            group = packed.at[g, rows_of(core * HALF + x * GROUP, GROUP)]
            sent.append(send(group, group, s4.at[g, a], r4.at[g, a], twin))

    def core_gather(g):
        for a in STEPS_X[::-1]:
            x = lax.rem(my_x + SIZE_X - a, SIZE_X)
            group = packed.at[g, rows_of((1 - core) * HALF + x * GROUP, GROUP)]
            arrived(group, s4.at[g, a], r4.at[g, a], twin)
        result = (grad_first, grad_second)[g]
        for tile in range(TILES_WIDE):
            for depth in range(3):
                at = tile * TALL + depth * CH
                block = packed[g, at : at + CH].astype(F32).T
                low = LANES * tile
                for pair in range(9):
                    begin, end = max(low, CH * pair), min(low + LANES, CH * (pair + 1))
                    if begin < end:
                        row = (3 * pair + depth) * CH + begin - CH * pair
                        result[row : row + end - begin] = block[begin - low : end - low]

    gradient(st, bx, 0, 1, False)
    core_send(0)
    gradient(ct, bh, 1, 0, False)
    core_send(1)
    core_add(0)
    core_add(1)

    for planes in ((0, 1, 2, 3), (4, 5, 6, 7), (8, 9, 10, 11), (12, 13, 14, 15)):
        start, count = planes[0], len(planes)
        total = convolve(bh, c2, planes, 0)
        inputs = fx[(start + AHEAD) * FACE : (start + AHEAD + count) * FACE]
        sums[start * FACE : (start + count) * FACE] = keep(total + inputs, planes)

    def place(n, carry):
        low = sums[pl.ds(pl.multiple_of(n * STEP, STEP), STEP)]
        high = sums[pl.ds(pl.multiple_of(ROWS // 2 + n * STEP, STEP), STEP)]
        for slot in range(2):
            chosen = jnp.where(down == slot, low, jnp.where(up == slot, high, 0.0))
            chosen = chosen.reshape(CHUNK, EDGE, EDGE, LANES)[..., :CH]
            out[slot, pl.ds(n * CHUNK, CHUNK)] = chosen.astype(BF16)
        return carry

    lax.fori_loop(0, 2, place, 0, unroll=True)

    for stage in (plane_add, line_add, plane_gather, core_gather):
        for g in range(2):
            stage(g)
    for copy in sent:
        copy.wait_send()
    for g in range(2):
        all_sent(plane_out.at[g], s1.at[g])
        all_sent(cross.at[g, : SIDE - 1], s2.at[g])
        all_sent(packed.at[g, : HALF - SHARD], s3.at[g])


def store(*refs):
    count = len(refs) // 2
    copies = [
        pltpu.make_async_copy(src, dst, refs[-1].at[n])
        for n, (src, dst) in enumerate(zip(refs[:count], refs[count : 2 * count]))
    ]
    for copy in copies:
        copy.start()
    for copy in copies:
        copy.wait()


def on_device(voxels, cotangent, weight_first, weight_second, act_count, up_list, down_list, table):
    vmem = pl.BlockSpec(memory_space=pltpu.VMEM)
    smem = pl.BlockSpec(memory_space=pltpu.SMEM)
    scale = 1.0 / math.sqrt(512 * 2 * EDGE**3)
    dma = pltpu.SemaphoreType.DMA
    field_shape = jax.ShapeDtypeStruct((2, EDGE, EDGE, EDGE, CH), BF16)
    sum_shape = jax.ShapeDtypeStruct((27 * CH, CH), F32)
    results = (field_shape, sum_shape, sum_shape)
    planes = [pltpu.VMEM((ROWS + 2 * n * FACE, LANES), F32) for n in (AHEAD, 1, 1)]
    wide = [pltpu.VMEM((ROWS + 2 * n * FACE, TILES_WIDE * LANES), BF16) for n in (1, 0, 0)]
    joined = pltpu.VMEM((WIDE, 3 * LANES), BF16)
    weight = pltpu.VMEM((27, CH, CH), BF16)
    bricks = pltpu.VMEM(field_shape.shape, BF16)
    turned = pltpu.VMEM((TALL, ROWS), BF16)
    held = pl.pallas_call(
        functools.partial(section, scale),
        out_shape=results,
        in_specs=[smem, smem] + [pl.BlockSpec(memory_space=pltpu.HBM)] * 4,
        out_specs=(vmem,) * 3,
        scratch_shapes=[
            bricks, bricks, weight, weight, *planes, *wide, joined, joined, joined,
            *[pltpu.VMEM((ROWS, LANES), F32)] * 3,
            turned, turned,
            *[pltpu.VMEM(((AHEAD + 1) * FACE + FLAG_ROWS, LANES), BF16)] * 4,
            pltpu.VMEM((2, 2 * HALF, LANES), F32),
            pltpu.VMEM((2, HALF, LANES), F32),
            *[pltpu.VMEM((2, len(PLANE), SHARD, LANES), BF16)] * 2,
            pltpu.VMEM((2, SHARD, LANES), F32),
            pltpu.VMEM((2, SIDE, SHARD, LANES), F32),
            pltpu.VMEM((2, 2 * HALF, LANES), BF16),
            dma((4,)), dma((2,)), dma((2,)),
            *[dma((2, SIZE_X))] * 2, *[dma((2,))] * 5, *[dma((2, SIZE_X))] * 3,
        ],
        compiler_params=pltpu.CompilerParams(
            collective_id=0, has_side_effects=True, vmem_limit_bytes=48 * 2**20
        ),
        name="section",
    )(
        down_list, up_list,
        *[
            pltpu.with_memory_space_constraint(array, pltpu.HBM)
            for array in (voxels[0], cotangent[0], weight_first, weight_second)
        ],
    )
    out_field, first, second = pl.pallas_call(
        store,
        out_shape=results,
        in_specs=[vmem] * 3,
        out_specs=(pl.BlockSpec(memory_space=pltpu.HBM),) * 3,
        scratch_shapes=[dma((3,))],
        compiler_params=pltpu.CompilerParams(vmem_limit_bytes=8 * 2**20),
        name="store",
    )(*held)
    shape = weight_first.shape
    return (out_field[None], first.reshape(shape), second.reshape(shape))


def solution(mesh):
    in_specs = (
        P("rep", "space", None, None, None, None),
        P("rep", "space", None, None, None, None),
        P(),
        P(),
        P("rep", "space"),
        P("rep", "space"),
        P("rep", "space"),
        P("rep", "space", None),
    )
    out_specs = (P("rep", "space", None, None, None, None), P(), P())
    return jax.shard_map(
        on_device, mesh=mesh, in_specs=in_specs, out_specs=out_specs, check_vma=False
    )
```

```python
import functools
import math

import jax
import jax.numpy as jnp
from jax import lax
from jax.experimental import pallas as pl
from jax.experimental.pallas import tpu as pltpu
from jax.sharding import PartitionSpec as P

F32 = jnp.float32
BF16 = jnp.bfloat16
MESH = pl.DeviceIdType.MESH

SIZE_X, SIZE_Y, SIZE_Z = 4, 8, 8
EDGE = 8
CH = 96
LANES = 128
FACE = EDGE * EDGE
PLANES = 2 * EDGE
ROWS = PLANES * FACE
WIDE = 9 * CH
TALL = 3 * CH
TILES_WIDE = 7
HALF = 1024
GROUP = HALF // SIZE_X
SIDE = 8
SHARD = GROUP // SIDE
STEPS_X = (2, 1, 3, 0)
STEPS = (4, 3, 5, 2, 6, 1, 7)
PLANE = tuple((a, b) for a in STEPS_X for b in STEPS + (0,) if a or b)
FLAG_ROWS = 16
AHEAD = 2
BLOCKS = (tuple(range(21)), tuple(range(11, 21)) + tuple(range(11)))
WHOLE = 10
CHUNK = 4
STEP = CHUNK * FACE


def widen(value):
    value = value.astype(F32)
    blank = jnp.zeros(value.shape[:-1] + (LANES - CH,), F32)
    return jnp.concatenate([value, blank], axis=-1)


def shifted(value, step):
    if step == 0:
        return value
    deep = value.reshape(-1, EDGE, LANES)
    depth = lax.broadcasted_iota(jnp.int32, deep.shape, 1)
    if step > 0:
        moved = jnp.where(depth == EDGE - 1, 0.0, pltpu.roll(deep, EDGE - 1, 1))
    else:
        moved = jnp.where(depth == 0, 0.0, pltpu.roll(deep, 1, 1))
    return moved.reshape(value.shape)


def spread(value, out, row):
    planes = value.shape[0] - 2
    flat = value.reshape(-1, LANES)
    turns = {turn: pltpu.roll(flat, turn, 1).reshape(value.shape) for turn in (32, 64, 96)}
    turns[0] = value

    def piece(index):
        shift_x, shift_y = index // 3, index % 3
        turned = turns[CH * index % LANES][shift_x : shift_x + planes]
        blank = jnp.zeros((planes, 1, EDGE, LANES), F32)
        if shift_y == 0:
            turned = jnp.concatenate([blank, turned[:, : EDGE - 1]], axis=1)
        elif shift_y == 2:
            turned = jnp.concatenate([turned[:, 1:], blank], axis=1)
        return turned.reshape(planes * FACE, LANES)

    lane = lax.broadcasted_iota(jnp.int32, (planes * FACE, LANES), 1)
    pieces = [piece(index) for index in range(9)]
    for tile in range(TILES_WIDE):
        first = LANES * tile // CH
        border = CH * (first + 1) - LANES * tile
        block = pieces[first]
        if border < LANES and first + 1 < 9:
            block = jnp.where(lane < border, block, pieces[first + 1])
        out[row : row + planes * FACE, LANES * tile : LANES * (tile + 1)] = block.astype(BF16)


def section(
    scale,
    down_ref, up_ref, vox_hbm, cot_hbm, w1_hbm, w2_hbm,
    out, grad_first, grad_second,
    vox, cot, w1, w2, fx, fh, fg, bx, bh, bg, c1, c2, ct2, dslope, slopes, sums, st, ct,
    up_send, down_send, from_lo, from_hi,
    part_sum, core_in, plane_out, plane_in, mid, cross, packed,
    load_s, halo_s, halo_r, s0, r0, s1, r1, s2, r2, s3, r3, s4, r4,
):
    space = lax.axis_index("space")
    rep = lax.axis_index("rep")
    owners = SIZE_X * SIZE_Z * 2
    y_lo = lax.rem(space, 2)
    my_z = lax.rem(lax.div(space, 2), SIZE_Z)
    my_x = lax.div(space, 2 * SIZE_Z)
    core = lax.rem(rep, 2)
    my_y = lax.div(rep, 2) * 2 + y_lo

    def device(x, y, z, c):
        return ((x * SIZE_Z + z) * 2 + lax.rem(y, 2), lax.div(y, 2) * 2 + c)

    side = my_z * (1 - core) + my_y * core
    line = my_y * (1 - core) + my_z * core

    def in_plane(x, t):
        return device(x, my_y * (1 - core) + t * core, t * (1 - core) + my_z * core, core)

    def in_line(t):
        return device(my_x, t * (1 - core) + my_y * core, my_z * (1 - core) + t * core, core)

    def moved(a, b):
        return lax.rem(my_x + a, SIZE_X), lax.rem(side + b, SIDE)

    twin = device(my_x, my_y, my_z, 1 - core)
    above = (lax.rem(space + 1, owners), rep)
    below = (lax.rem(space + owners - 1, owners), rep)

    def send(src, dst, send_sem, recv_sem, target):
        copy = pltpu.make_async_remote_copy(
            src_ref=src, dst_ref=dst, send_sem=send_sem, recv_sem=recv_sem,
            device_id=target, device_id_type=MESH,
        )
        copy.start()
        return copy

    def arrived(dst, send_sem, recv_sem, target):
        pltpu.make_async_remote_copy(
            src_ref=dst, dst_ref=dst, send_sem=send_sem, recv_sem=recv_sem,
            device_id=target, device_id_type=MESH,
        ).wait_recv()

    loads = [
        pltpu.make_async_copy(src, dst, load_s.at[n])
        for n, (src, dst) in enumerate(
            ((vox_hbm, vox), (cot_hbm, cot), (w1_hbm, w1), (w2_hbm, w2))
        )
    ]
    for load in loads[:2]:
        load.start()

    barrier = pltpu.get_barrier_semaphore()
    partners = [above, below, twin]
    partners += [in_plane(*moved(a, b)) for a, b in PLANE]
    partners += [in_line(lax.rem(line + d, SIDE)) for d in STEPS]
    for partner in partners:
        pl.semaphore_signal(barrier, inc=1, device_id=partner, device_id_type=MESH)

    for load in loads[2:]:
        load.start()
    down = down_ref[0, 0]
    up = up_ref[0, 0]
    sent = []
    for joined in (c1, c2, ct2):
        joined[...] = jnp.zeros(joined.shape, BF16)

    def fill(field, planes, ahead):
        for slot, start in ((down, 0), (up, EDGE)):
            for at in range(0, EDGE, CHUNK):
                one, two = (widen(field[n, at : at + CHUNK]) for n in range(2))
                chosen = jnp.where(slot == 0, one, jnp.where(slot == 1, two, 0.0))
                row = (ahead + start + at) * FACE
                planes[row : row + STEP] = chosen.reshape(STEP, LANES)

    loads[0].wait()
    fill(vox, fx, AHEAD)
    loads[1].wait()
    fill(cot, fg, 1)
    flags = (AHEAD + 1) * FACE
    for buffer, slot, high, low in (
        (up_send, up, PLANES - AHEAD, PLANES - 1), (down_send, down, 0, 0)
    ):
        row = (AHEAD + high) * FACE
        buffer[: AHEAD * FACE] = fx[row : row + AHEAD * FACE].astype(BF16)
        buffer[AHEAD * FACE : flags] = fg[(1 + low) * FACE : (2 + low) * FACE].astype(BF16)
        buffer[flags:] = jnp.where(slot < 2, 1.0, 0.0) * jnp.ones((FLAG_ROWS, LANES), BF16)
    pl.semaphore_wait(barrier, len(partners))
    sent.append(send(up_send, from_lo, halo_s.at[0], halo_r.at[0], above))
    sent.append(send(down_send, from_hi, halo_s.at[1], halo_r.at[1], below))

    def join(offset, value, joined):
        pair, depth = offset // 3, offset % 3
        joined[pair * CH : (pair + 1) * CH, LANES * depth : LANES * depth + CH] = value

    lower_valid = space > 0
    upper_valid = space < owners - 1

    def neighbour(buffer, valid):
        flag = buffer[flags : flags + FLAG_ROWS].astype(F32)[:1]
        return jnp.where(valid, flag, 0.0) > 0.5

    def keep(value, planes):
        kept = []
        for k, plane in enumerate(planes):
            if plane < 0:
                active = neighbour(from_lo, lower_valid)
            elif plane >= PLANES:
                active = neighbour(from_hi, upper_valid)
            else:
                active = (down if plane < EDGE else up) < 2
            kept.append(jnp.where(active, value[k * FACE : (k + 1) * FACE], 0.0))
        return jnp.concatenate(kept, axis=0)

    def runs(planes):
        found = []
        for k, plane in enumerate(planes):
            if k and plane == planes[k - 1] + 1:
                found[-1][2] += 1
            else:
                found.append([k, plane, 1])
        return found

    def widened(source, ahead, wide, wide_ahead, planes):
        for _, first, count in runs(planes):
            rows = slice((first - 1 + ahead) * FACE, (first + 1 + count + ahead) * FACE)
            value = source[rows].reshape(count + 2, EDGE, EDGE, LANES)
            spread(value, wide, (first + wide_ahead) * FACE)

    def convolve(wide, joined, planes, ahead):
        rows = [
            wide[(first + ahead) * FACE : (first + ahead + count) * FACE, :WIDE]
            for _, first, count in runs(planes)
        ]
        rows = rows[0] if len(rows) == 1 else jnp.concatenate(rows, axis=0)
        product = jnp.dot(rows, joined[...], preferred_element_type=F32)
        parts = [product[:, LANES * k : LANES * (k + 1)] for k in range(3)]
        return shifted(parts[0], -1) + parts[1] + shifted(parts[2], 1)

    def first_conv(planes):
        widened(fx, AHEAD, bx, 1, planes)
        before = keep(convolve(bx, c1, planes, 1), planes)
        gate = jax.nn.sigmoid(before)
        factor = gate * (1.0 + before * (1.0 - gate))
        hidden = (before * gate).astype(BF16).astype(F32)
        for k, plane in enumerate(planes):
            part = slice(k * FACE, (k + 1) * FACE)
            if 0 <= plane < PLANES:
                dslope[plane * FACE : (plane + 1) * FACE] = factor[part]
            fh[(plane + 1) * FACE : (plane + 2) * FACE] = hidden[part]

    def through(planes):
        widened(fg, 1, bg, 0, planes)
        total = keep(convolve(bg, ct2, planes, 0), planes)
        for k, first, count in runs(planes):
            rows = slice(first * FACE, (first + count) * FACE)
            slopes[rows] = total[k * FACE : (k + count) * FACE] * dslope[rows]

    def turn(source, ahead, turned, pairs):
        for pair in pairs:
            rows = slice(pair * 2 * FACE, (pair + 1) * 2 * FACE)
            value = source[(2 * pair + ahead) * FACE : (2 * pair + 2 + ahead) * FACE]
            for depth in range(3):
                block = shifted(value, 1 - depth).T[:CH]
                turned[depth * CH : (depth + 1) * CH, rows] = block.astype(BF16)

    def gradient(turned, wide, g, ahead, inside):
        def rows(plane, count):
            return slice((ahead + plane) * FACE, (ahead + plane + count) * FACE)

        if inside:
            left, right = turned[:, 2 * FACE : 14 * FACE], wide[rows(2, 12)]
        else:
            left = jnp.concatenate([turned[:, : 2 * FACE], turned[:, 14 * FACE :]], axis=1)
            right = jnp.concatenate([wide[rows(0, 2)], wide[rows(14, 2)]], axis=0)
        block = jnp.dot(left, right, preferred_element_type=F32)
        for tile in range(TILES_WIDE):
            at = slice(tile * TALL, (tile + 1) * TALL)
            part = block[:, LANES * tile : LANES * (tile + 1)]
            part_sum[g, at] = part if inside else part_sum[g, at] + part

    inner = ((1, 2, 3, 4), (5, 6, 7), (8, 9, 10), (11, 12, 13, 14))
    loads[2].wait()
    for offset in range(27):
        join(offset, w1[offset], c1)
    for planes in inner:
        first_conv(planes)
    loads[3].wait()
    for offset in range(27):
        own = widen(w2[offset])
        square = jnp.concatenate([own, jnp.zeros((LANES - CH, LANES), F32)], axis=0)
        join(26 - offset, square.T[:CH, :CH].astype(BF16), ct2)
    for planes in inner:
        through(planes)
    turn(fg, 1, ct, range(8))
    turn(slopes, 0, st, range(1, 7))
    for planes in ((2, 3, 4), (5, 6, 7), (8, 9, 10), (11, 12, 13)):
        widened(fh, 1, bh, 0, planes)
    used = TILES_WIDE * TALL
    for g in range(2):
        part_sum[g, used:] = jnp.zeros((2 * HALF - used, LANES), F32)
    gradient(st, bx, 0, 1, True)
    gradient(ct, bh, 1, 0, True)
    for offset in range(27):
        join(offset, w2[offset], c2)

    def edge_in(buffer, at, count, valid, planes, row):
        block = buffer[at * FACE : (at + count) * FACE].astype(F32)
        planes[row : row + count * FACE] = jnp.where(valid, block, 0.0)

    arrived(from_lo, halo_s.at[0], halo_r.at[0], above)
    arrived(from_hi, halo_s.at[1], halo_r.at[1], below)
    edge_in(from_lo, 0, AHEAD, lower_valid, fx, 0)
    edge_in(from_hi, 0, AHEAD, upper_valid, fx, (PLANES + AHEAD) * FACE)
    edge_in(from_lo, AHEAD, 1, lower_valid, fg, 0)
    edge_in(from_hi, AHEAD, 1, upper_valid, fg, (PLANES + 1) * FACE)
    first_conv((-1, 0, 15, 16))
    widened(fh, 1, bh, 0, (0, 1, 14, 15))

    def rows_of(start, count):
        return pl.ds(pl.multiple_of(start, SHARD), count)

    def other(k, me):
        return k + jnp.where(k >= me, 1, 0)

    def core_send(g):
        for a in STEPS_X:
            start = lax.rem(my_x + a, SIZE_X) * GROUP
            src = part_sum.at[g, rows_of((1 - core) * HALF + start, GROUP)]
            dst = core_in.at[g, rows_of(start, GROUP)]
            sent.append(send(src, dst, s0.at[g, a], r0.at[g, a], twin))

    def all_sent(src, sem):
        pltpu.make_async_copy(src, src, sem).wait()

    def core_add(g):
        for n, (a, b) in enumerate(PLANE):
            x, t = moved(a, b)
            if b == STEPS[0]:
                group = core_in.at[g, rows_of(x * GROUP, GROUP)]
                arrived(group, s0.at[g, a], r0.at[g, a], twin)
            at = x * GROUP + t * SHARD
            total = part_sum[g, rows_of(core * HALF + at, SHARD)] + core_in[g, rows_of(at, SHARD)]
            plane_out[g, n] = total.astype(BF16)
            send(plane_out.at[g, n], plane_in.at[g, n], s1.at[g], r1.at[g], in_plane(x, t))
        at = my_x * GROUP + side * SHARD
        mid[g] = part_sum[g, rows_of(core * HALF + at, SHARD)] + core_in[g, rows_of(at, SHARD)]

    def plane_add(g):
        arrived(plane_in.at[g], s1.at[g], r1.at[g], twin)
        total = mid[g]
        for n in range(len(PLANE)):
            total = total + plane_in[g, n].astype(F32)
        cross[g, line] = total
        mine = cross.at[g, line]
        for k in range(SIDE - 1):
            t = other(k, line) * core + lax.rem(line + STEPS[k], SIDE) * (1 - core)
            send(mine, mine, s2.at[g], r2.at[g], in_line(t))

    def line_add(g):
        arrived(cross.at[g, : SIDE - 1], s2.at[g], r2.at[g], twin)
        total = cross[g, 0]
        for t in range(1, SIDE):
            total = total + cross[g, t]
        rows = rows_of(core * HALF + my_x * GROUP + side * SHARD, SHARD)
        packed[g, rows] = (total * scale).astype(BF16)
        mine = packed.at[g, rows]
        me = side * SIZE_X + my_x
        for k in range(SIDE * SIZE_X - 1):
            at = other(k, me)
            x, t = moved(*PLANE[k])
            x = lax.rem(at, SIZE_X) * (1 - core) + x * core
            t = lax.div(at, SIZE_X) * (1 - core) + t * core
            target = in_plane(x, t)
            send(mine, mine, s3.at[g], r3.at[g, my_x], target)

    def plane_gather(g):
        for a in STEPS_X[::-1]:
            x = lax.rem(my_x + SIZE_X - a, SIZE_X)
            count = GROUP if a else GROUP - SHARD
            arrived(packed.at[g, rows_of(core * HALF + x * GROUP, count)], s3.at[g], r3.at[g, x], twin)
            group = packed.at[g, rows_of(core * HALF + x * GROUP, GROUP)]
            sent.append(send(group, group, s4.at[g, a], r4.at[g, a], twin))
        for c in range(2):
            pl.when(core == c)(functools.partial(results, g, BLOCKS[c][:WHOLE]))

    def core_gather(g):
        for a in STEPS_X[::-1]:
            x = lax.rem(my_x + SIZE_X - a, SIZE_X)
            group = packed.at[g, rows_of((1 - core) * HALF + x * GROUP, GROUP)]
            arrived(group, s4.at[g, a], r4.at[g, a], twin)
        for c in range(2):
            pl.when(core == c)(functools.partial(results, g, BLOCKS[c][WHOLE:]))

    def results(g, blocks):
        result = (grad_first, grad_second)[g]
        for n in blocks:
            block = packed[g, n * CH : (n + 1) * CH].astype(F32).T
            low = LANES * (n // 3)
            for pair in range(9):
                begin, end = max(low, CH * pair), min(low + LANES, CH * (pair + 1))
                if begin < end:
                    row = (3 * pair + n % 3) * CH + begin - CH * pair
                    result[row : row + end - begin] = block[begin - low : end - low]

    gradient(ct, bh, 1, 0, False)
    core_send(1)
    through((0, 15))
    turn(slopes, 0, st, (0, 7))
    gradient(st, bx, 0, 1, False)
    core_send(0)
    core_add(1)
    core_add(0)

    for planes in ((0, 1, 2, 3), (4, 5, 6, 7), (8, 9, 10, 11), (12, 13, 14, 15)):
        start, count = planes[0], len(planes)
        total = convolve(bh, c2, planes, 0)
        inputs = fx[(start + AHEAD) * FACE : (start + AHEAD + count) * FACE]
        sums[start * FACE : (start + count) * FACE] = keep(total + inputs, planes)

    def place(n, carry):
        low = sums[pl.ds(pl.multiple_of(n * STEP, STEP), STEP)]
        high = sums[pl.ds(pl.multiple_of(ROWS // 2 + n * STEP, STEP), STEP)]
        for slot in range(2):
            chosen = jnp.where(down == slot, low, jnp.where(up == slot, high, 0.0))
            chosen = chosen.reshape(CHUNK, EDGE, EDGE, LANES)[..., :CH]
            out[slot, pl.ds(n * CHUNK, CHUNK)] = chosen.astype(BF16)
        return carry

    lax.fori_loop(0, 2, place, 0, unroll=True)

    for stage in (plane_add, line_add, plane_gather, core_gather):
        for g in (1, 0):
            stage(g)
    for copy in sent:
        copy.wait_send()
    for g in range(2):
        all_sent(plane_out.at[g], s1.at[g])
        all_sent(cross.at[g, : SIDE - 1], s2.at[g])
        all_sent(packed.at[g, : HALF - SHARD], s3.at[g])


def store(*refs):
    count = len(refs) // 2
    copies = [
        pltpu.make_async_copy(src, dst, refs[-1].at[n])
        for n, (src, dst) in enumerate(zip(refs[:count], refs[count : 2 * count]))
    ]
    for copy in copies:
        copy.start()
    for copy in copies:
        copy.wait()


def on_device(voxels, cotangent, weight_first, weight_second, act_count, up_list, down_list, table):
    vmem = pl.BlockSpec(memory_space=pltpu.VMEM)
    smem = pl.BlockSpec(memory_space=pltpu.SMEM)
    scale = 1.0 / math.sqrt(512 * 2 * EDGE**3)
    dma = pltpu.SemaphoreType.DMA
    field_shape = jax.ShapeDtypeStruct((2, EDGE, EDGE, EDGE, CH), BF16)
    sum_shape = jax.ShapeDtypeStruct((27 * CH, CH), F32)
    results = (field_shape, sum_shape, sum_shape)
    planes = [pltpu.VMEM((ROWS + 2 * n * FACE, LANES), F32) for n in (AHEAD, 1, 1)]
    wide = [pltpu.VMEM((ROWS + 2 * n * FACE, TILES_WIDE * LANES), BF16) for n in (1, 0, 0)]
    joined = pltpu.VMEM((WIDE, 3 * LANES), BF16)
    weight = pltpu.VMEM((27, CH, CH), BF16)
    bricks = pltpu.VMEM(field_shape.shape, BF16)
    turned = pltpu.VMEM((TALL, ROWS), BF16)
    held = pl.pallas_call(
        functools.partial(section, scale),
        out_shape=results,
        in_specs=[smem, smem] + [pl.BlockSpec(memory_space=pltpu.HBM)] * 4,
        out_specs=(vmem,) * 3,
        scratch_shapes=[
            bricks, bricks, weight, weight, *planes, *wide, joined, joined, joined,
            *[pltpu.VMEM((ROWS, LANES), F32)] * 3,
            turned, turned,
            *[pltpu.VMEM(((AHEAD + 1) * FACE + FLAG_ROWS, LANES), BF16)] * 4,
            pltpu.VMEM((2, 2 * HALF, LANES), F32),
            pltpu.VMEM((2, HALF, LANES), F32),
            *[pltpu.VMEM((2, len(PLANE), SHARD, LANES), BF16)] * 2,
            pltpu.VMEM((2, SHARD, LANES), F32),
            pltpu.VMEM((2, SIDE, SHARD, LANES), F32),
            pltpu.VMEM((2, 2 * HALF, LANES), BF16),
            dma((4,)), dma((2,)), dma((2,)),
            *[dma((2, SIZE_X))] * 2, *[dma((2,))] * 5, *[dma((2, SIZE_X))] * 3,
        ],
        compiler_params=pltpu.CompilerParams(
            collective_id=0, has_side_effects=True, vmem_limit_bytes=48 * 2**20
        ),
        name="section",
    )(
        down_list, up_list,
        *[
            pltpu.with_memory_space_constraint(array, pltpu.HBM)
            for array in (voxels[0], cotangent[0], weight_first, weight_second)
        ],
    )
    out_field, first, second = pl.pallas_call(
        store,
        out_shape=results,
        in_specs=[vmem] * 3,
        out_specs=(pl.BlockSpec(memory_space=pltpu.HBM),) * 3,
        scratch_shapes=[dma((3,))],
        compiler_params=pltpu.CompilerParams(vmem_limit_bytes=8 * 2**20),
        name="store",
    )(*held)
    shape = weight_first.shape
    return (out_field[None], first.reshape(shape), second.reshape(shape))


def solution(mesh):
    in_specs = (
        P("rep", "space", None, None, None, None),
        P("rep", "space", None, None, None, None),
        P(),
        P(),
        P("rep", "space"),
        P("rep", "space"),
        P("rep", "space"),
        P("rep", "space", None),
    )
    out_specs = (P("rep", "space", None, None, None, None), P(), P())
    return jax.shard_map(
        on_device, mesh=mesh, in_specs=in_specs, out_specs=out_specs, check_vma=False
    )
```

```python
import functools
import math

import jax
import jax.numpy as jnp
from jax import lax
from jax.experimental import pallas as pl
from jax.experimental.pallas import tpu as pltpu
from jax.sharding import PartitionSpec as P

F32 = jnp.float32
BF16 = jnp.bfloat16
MESH = pl.DeviceIdType.MESH

SIZE_X, SIZE_Y, SIZE_Z = 4, 8, 8
EDGE = 8
CH = 96
LANES = 128
FACE = EDGE * EDGE
PLANES = 2 * EDGE
ROWS = PLANES * FACE
WIDE = 9 * CH
TALL = 3 * CH
TILES_WIDE = 7
HALF = 1024
GROUP = HALF // SIZE_X
SIDE = 8
SHARD = GROUP // SIDE
STEPS_X = (2, 1, 3, 0)
STEPS = (4, 3, 5, 2, 6, 1, 7)
PLANE = tuple((a, b) for a in STEPS_X for b in STEPS + (0,) if a or b)
FLAG_ROWS = 16
AHEAD = 2
CHUNK = 4
STEP = CHUNK * FACE


def widen(value):
    value = value.astype(F32)
    blank = jnp.zeros(value.shape[:-1] + (LANES - CH,), F32)
    return jnp.concatenate([value, blank], axis=-1)


def shifted(value, step):
    if step == 0:
        return value
    deep = value.reshape(-1, EDGE, LANES)
    depth = lax.broadcasted_iota(jnp.int32, deep.shape, 1)
    if step > 0:
        moved = jnp.where(depth == EDGE - 1, 0.0, pltpu.roll(deep, EDGE - 1, 1))
    else:
        moved = jnp.where(depth == 0, 0.0, pltpu.roll(deep, 1, 1))
    return moved.reshape(value.shape)


def spread(value, out, row):
    planes = value.shape[0] - 2
    flat = value.reshape(-1, LANES)
    turns = {turn: pltpu.roll(flat, turn, 1).reshape(value.shape) for turn in (32, 64, 96)}
    turns[0] = value

    def piece(index):
        shift_x, shift_y = index // 3, index % 3
        turned = turns[CH * index % LANES][shift_x : shift_x + planes]
        blank = jnp.zeros((planes, 1, EDGE, LANES), F32)
        if shift_y == 0:
            turned = jnp.concatenate([blank, turned[:, : EDGE - 1]], axis=1)
        elif shift_y == 2:
            turned = jnp.concatenate([turned[:, 1:], blank], axis=1)
        return turned.reshape(planes * FACE, LANES)

    lane = lax.broadcasted_iota(jnp.int32, (planes * FACE, LANES), 1)
    pieces = [piece(index) for index in range(9)]
    for tile in range(TILES_WIDE):
        first = LANES * tile // CH
        border = CH * (first + 1) - LANES * tile
        block = pieces[first]
        if border < LANES and first + 1 < 9:
            block = jnp.where(lane < border, block, pieces[first + 1])
        out[row : row + planes * FACE, LANES * tile : LANES * (tile + 1)] = block.astype(BF16)


def section(
    scale,
    down_ref, up_ref, vox_hbm, cot_hbm, w1_hbm, w2_hbm,
    out, grad_first, grad_second,
    vox, cot, w1, w2, fx, fh, fg, bx, bh, bg, c1, c2, ct2, dslope, slopes, sums, st, ct,
    up_send, down_send, from_lo, from_hi,
    part_sum, core_in, plane_out, plane_in, mid, cross, packed,
    load_s, halo_s, halo_r, s0, r0, s1, r1, s2, r2, s3, r3, s4, r4,
):
    space = lax.axis_index("space")
    rep = lax.axis_index("rep")
    owners = SIZE_X * SIZE_Z * 2
    y_lo = lax.rem(space, 2)
    my_z = lax.rem(lax.div(space, 2), SIZE_Z)
    my_x = lax.div(space, 2 * SIZE_Z)
    core = lax.rem(rep, 2)
    my_y = lax.div(rep, 2) * 2 + y_lo

    def device(x, y, z, c):
        return ((x * SIZE_Z + z) * 2 + lax.rem(y, 2), lax.div(y, 2) * 2 + c)

    side = my_z * (1 - core) + my_y * core
    line = my_y * (1 - core) + my_z * core

    def in_plane(x, t):
        return device(x, my_y * (1 - core) + t * core, t * (1 - core) + my_z * core, core)

    def in_line(t):
        return device(my_x, t * (1 - core) + my_y * core, my_z * (1 - core) + t * core, core)

    def moved(a, b):
        return lax.rem(my_x + a, SIZE_X), lax.rem(side + b, SIDE)

    twin = device(my_x, my_y, my_z, 1 - core)
    above = (lax.rem(space + 1, owners), rep)
    below = (lax.rem(space + owners - 1, owners), rep)

    def send(src, dst, send_sem, recv_sem, target):
        copy = pltpu.make_async_remote_copy(
            src_ref=src, dst_ref=dst, send_sem=send_sem, recv_sem=recv_sem,
            device_id=target, device_id_type=MESH,
        )
        copy.start()
        return copy

    def arrived(dst, send_sem, recv_sem, target):
        pltpu.make_async_remote_copy(
            src_ref=dst, dst_ref=dst, send_sem=send_sem, recv_sem=recv_sem,
            device_id=target, device_id_type=MESH,
        ).wait_recv()

    loads = [
        pltpu.make_async_copy(src, dst, load_s.at[n])
        for n, (src, dst) in enumerate(
            ((vox_hbm, vox), (cot_hbm, cot), (w1_hbm, w1), (w2_hbm, w2))
        )
    ]
    for load in loads[:2]:
        load.start()

    barrier = pltpu.get_barrier_semaphore()
    partners = [above, below, twin]
    partners += [in_plane(*moved(a, b)) for a, b in PLANE]
    partners += [in_line(lax.rem(line + d, SIDE)) for d in STEPS]
    for partner in partners:
        pl.semaphore_signal(barrier, inc=1, device_id=partner, device_id_type=MESH)

    for load in loads[2:]:
        load.start()
    down = down_ref[0, 0]
    up = up_ref[0, 0]
    sent = []
    for joined in (c1, c2, ct2):
        joined[...] = jnp.zeros(joined.shape, BF16)

    def fill(field, planes, ahead):
        for slot, start in ((down, 0), (up, EDGE)):
            for at in range(0, EDGE, CHUNK):
                one, two = (widen(field[n, at : at + CHUNK]) for n in range(2))
                chosen = jnp.where(slot == 0, one, jnp.where(slot == 1, two, 0.0))
                row = (ahead + start + at) * FACE
                planes[row : row + STEP] = chosen.reshape(STEP, LANES)

    loads[0].wait()
    fill(vox, fx, AHEAD)
    loads[1].wait()
    fill(cot, fg, 1)
    flags = (AHEAD + 1) * FACE
    for buffer, slot, high, low in (
        (up_send, up, PLANES - AHEAD, PLANES - 1), (down_send, down, 0, 0)
    ):
        row = (AHEAD + high) * FACE
        buffer[: AHEAD * FACE] = fx[row : row + AHEAD * FACE].astype(BF16)
        buffer[AHEAD * FACE : flags] = fg[(1 + low) * FACE : (2 + low) * FACE].astype(BF16)
        buffer[flags:] = jnp.where(slot < 2, 1.0, 0.0) * jnp.ones((FLAG_ROWS, LANES), BF16)
    pl.semaphore_wait(barrier, len(partners))
    sent.append(send(up_send, from_lo, halo_s.at[0], halo_r.at[0], above))
    sent.append(send(down_send, from_hi, halo_s.at[1], halo_r.at[1], below))

    def join(offset, value, joined):
        pair, depth = offset // 3, offset % 3
        joined[pair * CH : (pair + 1) * CH, LANES * depth : LANES * depth + CH] = value

    lower_valid = space > 0
    upper_valid = space < owners - 1

    def neighbour(buffer, valid):
        flag = buffer[flags : flags + FLAG_ROWS].astype(F32)[:1]
        return jnp.where(valid, flag, 0.0) > 0.5

    def keep(value, planes):
        kept = []
        for k, plane in enumerate(planes):
            if plane < 0:
                active = neighbour(from_lo, lower_valid)
            elif plane >= PLANES:
                active = neighbour(from_hi, upper_valid)
            else:
                active = (down if plane < EDGE else up) < 2
            kept.append(jnp.where(active, value[k * FACE : (k + 1) * FACE], 0.0))
        return jnp.concatenate(kept, axis=0)

    def runs(planes):
        found = []
        for k, plane in enumerate(planes):
            if k and plane == planes[k - 1] + 1:
                found[-1][2] += 1
            else:
                found.append([k, plane, 1])
        return found

    def widened(source, ahead, wide, wide_ahead, planes):
        for _, first, count in runs(planes):
            rows = slice((first - 1 + ahead) * FACE, (first + 1 + count + ahead) * FACE)
            value = source[rows].reshape(count + 2, EDGE, EDGE, LANES)
            spread(value, wide, (first + wide_ahead) * FACE)

    def convolve(wide, joined, planes, ahead):
        rows = [
            wide[(first + ahead) * FACE : (first + ahead + count) * FACE, :WIDE]
            for _, first, count in runs(planes)
        ]
        rows = rows[0] if len(rows) == 1 else jnp.concatenate(rows, axis=0)
        product = jnp.dot(rows, joined[...], preferred_element_type=F32)
        parts = [product[:, LANES * k : LANES * (k + 1)] for k in range(3)]
        return shifted(parts[0], -1) + parts[1] + shifted(parts[2], 1)

    def first_conv(planes):
        widened(fx, AHEAD, bx, 1, planes)
        before = keep(convolve(bx, c1, planes, 1), planes)
        gate = jax.nn.sigmoid(before)
        factor = gate * (1.0 + before * (1.0 - gate))
        hidden = (before * gate).astype(BF16).astype(F32)
        for k, plane in enumerate(planes):
            part = slice(k * FACE, (k + 1) * FACE)
            if 0 <= plane < PLANES:
                dslope[plane * FACE : (plane + 1) * FACE] = factor[part]
            fh[(plane + 1) * FACE : (plane + 2) * FACE] = hidden[part]

    def through(planes):
        widened(fg, 1, bg, 0, planes)
        total = keep(convolve(bg, ct2, planes, 0), planes)
        for k, first, count in runs(planes):
            rows = slice(first * FACE, (first + count) * FACE)
            slopes[rows] = total[k * FACE : (k + count) * FACE] * dslope[rows]

    def turn(source, ahead, turned, pairs):
        for pair in pairs:
            rows = slice(pair * 2 * FACE, (pair + 1) * 2 * FACE)
            value = source[(2 * pair + ahead) * FACE : (2 * pair + 2 + ahead) * FACE]
            for depth in range(3):
                block = shifted(value, 1 - depth).T[:CH]
                turned[depth * CH : (depth + 1) * CH, rows] = block.astype(BF16)

    def gradient(turned, wide, g, ahead, inside):
        def rows(plane, count):
            return slice((ahead + plane) * FACE, (ahead + plane + count) * FACE)

        if inside:
            left, right = turned[:, 2 * FACE : 14 * FACE], wide[rows(2, 12)]
        else:
            left = jnp.concatenate([turned[:, : 2 * FACE], turned[:, 14 * FACE :]], axis=1)
            right = jnp.concatenate([wide[rows(0, 2)], wide[rows(14, 2)]], axis=0)
        block = jnp.dot(left, right, preferred_element_type=F32)
        for tile in range(TILES_WIDE):
            at = slice(tile * TALL, (tile + 1) * TALL)
            part = block[:, LANES * tile : LANES * (tile + 1)]
            part_sum[g, at] = part if inside else part_sum[g, at] + part

    inner = ((1, 2, 3, 4), (5, 6, 7), (8, 9, 10), (11, 12, 13, 14))
    loads[2].wait()
    for offset in range(27):
        join(offset, w1[offset], c1)
    for planes in inner:
        first_conv(planes)
    loads[3].wait()
    for offset in range(27):
        own = widen(w2[offset])
        square = jnp.concatenate([own, jnp.zeros((LANES - CH, LANES), F32)], axis=0)
        join(26 - offset, square.T[:CH, :CH].astype(BF16), ct2)
    for planes in inner:
        through(planes)
    turn(fg, 1, ct, range(8))
    turn(slopes, 0, st, range(1, 7))
    for planes in ((2, 3, 4), (5, 6, 7), (8, 9, 10), (11, 12, 13)):
        widened(fh, 1, bh, 0, planes)
    used = TILES_WIDE * TALL
    for g in range(2):
        part_sum[g, used:] = jnp.zeros((2 * HALF - used, LANES), F32)
    gradient(st, bx, 0, 1, True)
    gradient(ct, bh, 1, 0, True)
    for offset in range(27):
        join(offset, w2[offset], c2)

    def edge_in(buffer, at, count, valid, planes, row):
        block = buffer[at * FACE : (at + count) * FACE].astype(F32)
        planes[row : row + count * FACE] = jnp.where(valid, block, 0.0)

    arrived(from_lo, halo_s.at[0], halo_r.at[0], above)
    arrived(from_hi, halo_s.at[1], halo_r.at[1], below)
    edge_in(from_lo, 0, AHEAD, lower_valid, fx, 0)
    edge_in(from_hi, 0, AHEAD, upper_valid, fx, (PLANES + AHEAD) * FACE)
    edge_in(from_lo, AHEAD, 1, lower_valid, fg, 0)
    edge_in(from_hi, AHEAD, 1, upper_valid, fg, (PLANES + 1) * FACE)
    first_conv((-1, 0, 15, 16))
    through((0, 15))
    turn(slopes, 0, st, (0, 7))
    widened(fh, 1, bh, 0, (0, 1, 14, 15))

    def rows_of(start, count):
        return pl.ds(pl.multiple_of(start, SHARD), count)

    def other(k, me):
        return k + jnp.where(k >= me, 1, 0)

    def core_send(g):
        for a in STEPS_X:
            start = lax.rem(my_x + a, SIZE_X) * GROUP
            src = part_sum.at[g, rows_of((1 - core) * HALF + start, GROUP)]
            dst = core_in.at[g, rows_of(start, GROUP)]
            send(src, dst, s0.at[g], r0.at[g, a], twin)

    def all_sent(src, sem):
        pltpu.make_async_copy(src, src, sem).wait()

    def core_add(g):
        for n, (a, b) in enumerate(PLANE):
            x, t = moved(a, b)
            if b == STEPS[0]:
                group = core_in.at[g, rows_of(x * GROUP, GROUP)]
                arrived(group, s0.at[g], r0.at[g, a], twin)
            at = x * GROUP + t * SHARD
            total = part_sum[g, rows_of(core * HALF + at, SHARD)] + core_in[g, rows_of(at, SHARD)]
            plane_out[g, n] = total.astype(BF16)
            send(plane_out.at[g, n], plane_in.at[g, n], s1.at[g], r1.at[g], in_plane(x, t))
        at = my_x * GROUP + side * SHARD
        mid[g] = part_sum[g, rows_of(core * HALF + at, SHARD)] + core_in[g, rows_of(at, SHARD)]

    def plane_add(g):
        arrived(plane_in.at[g], s1.at[g], r1.at[g], twin)
        total = mid[g]
        for n in range(len(PLANE)):
            total = total + plane_in[g, n].astype(F32)
        cross[g, line] = total
        mine = cross.at[g, line]
        for k in range(SIDE - 1):
            send(mine, mine, s2.at[g], r2.at[g], in_line(other(k, line)))

    def line_add(g):
        arrived(cross.at[g, : SIDE - 1], s2.at[g], r2.at[g], twin)
        total = cross[g, 0]
        for t in range(1, SIDE):
            total = total + cross[g, t]
        rows = rows_of(core * HALF + my_x * GROUP + side * SHARD, SHARD)
        packed[g, rows] = (total * scale).astype(BF16)
        mine = packed.at[g, rows]
        for t in range(SIDE):
            for a in STEPS_X[: 3 + (t < SIDE - 1)]:
                target = in_plane(moved(a, 0)[0], t if a else other(t, side))
                send(mine, mine, s3.at[g], r3.at[g, my_x], target)

    def plane_gather(g):
        for a in STEPS_X[::-1]:
            x = lax.rem(my_x + SIZE_X - a, SIZE_X)
            count = GROUP if a else GROUP - SHARD
            arrived(packed.at[g, rows_of(core * HALF + x * GROUP, count)], s3.at[g], r3.at[g, x], twin)
            group = packed.at[g, rows_of(core * HALF + x * GROUP, GROUP)]
            send(group, group, s4.at[g], r4.at[g, a], twin)

    def core_gather(g):
        for a in STEPS_X[::-1]:
            x = lax.rem(my_x + SIZE_X - a, SIZE_X)
            group = packed.at[g, rows_of((1 - core) * HALF + x * GROUP, GROUP)]
            arrived(group, s4.at[g], r4.at[g, a], twin)
        result = (grad_first, grad_second)[g]
        for tile in range(TILES_WIDE):
            for depth in range(3):
                at = tile * TALL + depth * CH
                block = packed[g, at : at + CH].astype(F32).T
                low = LANES * tile
                for pair in range(9):
                    begin, end = max(low, CH * pair), min(low + LANES, CH * (pair + 1))
                    if begin < end:
                        row = (3 * pair + depth) * CH + begin - CH * pair
                        result[row : row + end - begin] = block[begin - low : end - low]

    gradient(st, bx, 0, 1, False)
    core_send(0)
    gradient(ct, bh, 1, 0, False)
    core_send(1)
    core_add(0)
    core_add(1)

    for planes in ((0, 1, 2, 3), (4, 5, 6, 7), (8, 9, 10, 11), (12, 13, 14, 15)):
        start, count = planes[0], len(planes)
        total = convolve(bh, c2, planes, 0)
        inputs = fx[(start + AHEAD) * FACE : (start + AHEAD + count) * FACE]
        sums[start * FACE : (start + count) * FACE] = keep(total + inputs, planes)

    def place(n, carry):
        low = sums[pl.ds(pl.multiple_of(n * STEP, STEP), STEP)]
        high = sums[pl.ds(pl.multiple_of(ROWS // 2 + n * STEP, STEP), STEP)]
        for slot in range(2):
            chosen = jnp.where(down == slot, low, jnp.where(up == slot, high, 0.0))
            chosen = chosen.reshape(CHUNK, EDGE, EDGE, LANES)[..., :CH]
            out[slot, pl.ds(n * CHUNK, CHUNK)] = chosen.astype(BF16)
        return carry

    lax.fori_loop(0, 2, place, 0, unroll=True)

    for stage in (plane_add, line_add, plane_gather, core_gather):
        for g in range(2):
            stage(g)
    for copy in sent:
        copy.wait_send()
    for g in range(2):
        all_sent(part_sum.at[g, :HALF], s0.at[g])
        all_sent(plane_out.at[g], s1.at[g])
        all_sent(cross.at[g, : SIDE - 1], s2.at[g])
        all_sent(packed.at[g, : HALF - SHARD], s3.at[g])
        all_sent(packed.at[g, :HALF], s4.at[g])


def store(*refs):
    count = len(refs) // 2
    copies = [
        pltpu.make_async_copy(src, dst, refs[-1].at[n])
        for n, (src, dst) in enumerate(zip(refs[:count], refs[count : 2 * count]))
    ]
    for copy in copies:
        copy.start()
    for copy in copies:
        copy.wait()


def on_device(voxels, cotangent, weight_first, weight_second, act_count, up_list, down_list, table):
    vmem = pl.BlockSpec(memory_space=pltpu.VMEM)
    smem = pl.BlockSpec(memory_space=pltpu.SMEM)
    scale = 1.0 / math.sqrt(512 * 2 * EDGE**3)
    dma = pltpu.SemaphoreType.DMA
    field_shape = jax.ShapeDtypeStruct((2, EDGE, EDGE, EDGE, CH), BF16)
    sum_shape = jax.ShapeDtypeStruct((27 * CH, CH), F32)
    results = (field_shape, sum_shape, sum_shape)
    planes = [pltpu.VMEM((ROWS + 2 * n * FACE, LANES), F32) for n in (AHEAD, 1, 1)]
    wide = [pltpu.VMEM((ROWS + 2 * n * FACE, TILES_WIDE * LANES), BF16) for n in (1, 0, 0)]
    joined = pltpu.VMEM((WIDE, 3 * LANES), BF16)
    weight = pltpu.VMEM((27, CH, CH), BF16)
    bricks = pltpu.VMEM(field_shape.shape, BF16)
    turned = pltpu.VMEM((TALL, ROWS), BF16)
    held = pl.pallas_call(
        functools.partial(section, scale),
        out_shape=results,
        in_specs=[smem, smem] + [pl.BlockSpec(memory_space=pltpu.HBM)] * 4,
        out_specs=(vmem,) * 3,
        scratch_shapes=[
            bricks, bricks, weight, weight, *planes, *wide, joined, joined, joined,
            *[pltpu.VMEM((ROWS, LANES), F32)] * 3,
            turned, turned,
            *[pltpu.VMEM(((AHEAD + 1) * FACE + FLAG_ROWS, LANES), BF16)] * 4,
            pltpu.VMEM((2, 2 * HALF, LANES), F32),
            pltpu.VMEM((2, HALF, LANES), F32),
            *[pltpu.VMEM((2, len(PLANE), SHARD, LANES), BF16)] * 2,
            pltpu.VMEM((2, SHARD, LANES), F32),
            pltpu.VMEM((2, SIDE, SHARD, LANES), F32),
            pltpu.VMEM((2, 2 * HALF, LANES), BF16),
            dma((4,)), dma((2,)), dma((2,)),
            dma((2,)), dma((2, SIZE_X)), *[dma((2,))] * 5, dma((2, SIZE_X)), dma((2,)), dma((2, SIZE_X)),
        ],
        compiler_params=pltpu.CompilerParams(
            collective_id=0, has_side_effects=True, vmem_limit_bytes=48 * 2**20
        ),
        name="section",
    )(
        down_list, up_list,
        *[
            pltpu.with_memory_space_constraint(array, pltpu.HBM)
            for array in (voxels[0], cotangent[0], weight_first, weight_second)
        ],
    )
    out_field, first, second = pl.pallas_call(
        store,
        out_shape=results,
        in_specs=[vmem] * 3,
        out_specs=(pl.BlockSpec(memory_space=pltpu.HBM),) * 3,
        scratch_shapes=[dma((3,))],
        compiler_params=pltpu.CompilerParams(vmem_limit_bytes=8 * 2**20),
        name="store",
    )(*held)
    shape = weight_first.shape
    return (out_field[None], first.reshape(shape), second.reshape(shape))


def solution(mesh):
    in_specs = (
        P("rep", "space", None, None, None, None),
        P("rep", "space", None, None, None, None),
        P(),
        P(),
        P("rep", "space"),
        P("rep", "space"),
        P("rep", "space"),
        P("rep", "space", None),
    )
    out_specs = (P("rep", "space", None, None, None, None), P(), P())
    return jax.shard_map(
        on_device, mesh=mesh, in_specs=in_specs, out_specs=out_specs, check_vma=False
    )
```
